32 devices in a mesh: frames: 16 (over z, y, x), coils: 2 (over core).
Axes of the slice: x: 2, y: 2, z: 4, core: 2. Of those that a mesh axis runs over, the one named last changes fastest.
Arguments:
- kspace: bfloat16 [16, 8, 2, 32, 256], P('frames', 'coils'), may hold values from -6 to 6
- sensitivity: bfloat16 [8, 2, 256, 256], P('coils'), may hold values from -3 to 3
- spoke_count: int32 [16], P('frames'), may hold values from 1 to 32, 384 in all
- spoke_index: int32 [16, 32], P('frames'), may hold values from 0 to 32767
- band_offset: int32 [16, 32], P('frames'), may hold values from 0 to 252
- owner_map: int32 [2, 32768], replicated, may hold values from 0 to 32767, each once within a row
- aif: float32 [16], replicated, may hold values from 0.2 to 5
- ktrans: float32 [2, 32768], P('coils', 'frames'), may hold values from 0.02 to 0.4
- kep: float32 [2, 32768], P('coils', 'frames'), may hold values from 0.1 to 2
- baseline: float32 [2, 2, 32768], P(None, 'coils', 'frames'), may hold values from 0.5 to 2
Outputs:
- ktrans_new: float32 [2, 32768], P('coils', 'frames')
- kep_new: float32 [2, 32768], P('coils', 'frames')
- residual_images: bfloat16 [16, 2, 256, 256], P('frames', None, 'coils')
The draws below stay inside these ranges and needn't reach their ends.
Inputs may be any that keep to these rules, and one draw needn't show every extreme that they name: `spoke_count`: spoke counts of all frames sum to 384; some frame uses all 32 slots. `owner_map`: each row is a permutation of 0 to 32767.
All inputs are finite; a program needn't handle non-finite values. No bound on the sum of `spoke_count` on one device may be relied on, other than what follows from the above.
Results may differ from the reference program's by a relative error of at most 0.0074.
Values may be sent and summed in bfloat16 or wider, within the bound.
A program may use at most 64 MiB of HBM per device.

```python
import math
import jax
import jax.numpy as jnp
import numpy as np
from jax import lax

NX = 256
SPK = 32
BAND = 4
FRAMES = 16
COILS = 8
SLAB_VOX = 32768
SPOKE_TOTAL = 384
N_COILS = 2


def place_ends(values, rng, least, high):
    spot = [jax.random.randint(jax.random.fold_in(rng, axis), (), 0, length) for axis, length in enumerate(values.shape)]
    longest = values.shape.index(max(values.shape))
    neighbour = spot[:longest] + [(spot[longest] + 1) % values.shape[longest]] + spot[longest + 1:]
    return values.at[tuple(spot)].set(least).at[tuple(neighbour)].set(high)


def levels(rng, dims, shards, least, largest):
    loudness = 1.0
    for axis_at, parts in shards:
        steps = jax.random.uniform(jax.random.fold_in(jax.random.fold_in(rng, 6), axis_at), (parts,), jnp.float32, least / len(shards), largest / len(shards))
        loudness = loudness * jnp.repeat(jnp.exp(steps), dims[axis_at] // parts).reshape((-1,) + (1,) * (len(dims) - 1 - axis_at))
    return loudness


def length_profile(number_of, total, most, skew):
    loads = [(1 << 20) // math.isqrt(grade ** skew) + 1 for grade in range(2, number_of + 1)]
    surplus, counts = total - most - (number_of - 1), [1] * (number_of - 1)
    while surplus > 0:
        movable = [i for i in range(number_of - 1) if counts[i] < most]
        mass, budget = sum([loads[i] for i in movable]), surplus
        for i in movable:
            more = min(most - counts[i], max(1, budget * loads[i] // mass), surplus)
            counts[i] = counts[i] + more
            surplus = surplus - more
    return np.array([most] + counts)


def uneven(key, number_of, total, limit, lean):
    if number_of == 2:
        one = jax.random.randint(key, (), max(1, total - limit), min(limit, total - 1) + 1)
        return jnp.stack([one, total - one])
    tallies = jnp.asarray(length_profile(number_of, total, limit, lean), jnp.int32)
    twos = (number_of - 1) // 2
    donor, sink = tallies[1:1 + 2 * twos:2], tallies[2:2 + 2 * twos:2]
    margin = jnp.minimum(donor - 1, limit - sink)
    moved = jax.random.randint(jax.random.fold_in(key, 1), (twos,), 0, 1 << 20) % (margin + 1)
    tallies = tallies.at[1:1 + 2 * twos:2].set(donor - moved).at[2:2 + 2 * twos:2].set(sink + moved)
    return tallies[jax.random.permutation(jax.random.fold_in(key, 2), number_of)]


def scatter_about(key, extent, width, limit, cuts=(), kind=jnp.bfloat16):
    factor_of = levels(key, extent, cuts, -0.22, 0.18) if cuts else 1.0
    result = jax.random.normal(key, extent, jnp.float32) * width * factor_of
    return jnp.minimum(jnp.maximum(result, -limit), limit).astype(kind)


def setup_inputs(seed: int = 0) -> dict:
    arg_keys = jax.random.split(jax.random.key(seed), 11)
    kspace = scatter_about(arg_keys[0], (FRAMES, COILS, 2, SPK, NX), 1.0, 6.0, ((0, 16), (1, 2)))
    sensitivity = scatter_about(arg_keys[1], (COILS, 2, NX, NX), 0.5, 3.0, ((0, 2),))
    spoke_count = uneven(arg_keys[2], FRAMES, SPOKE_TOTAL, SPK, 2).astype(jnp.int32)
    spoke_index = place_ends(jax.random.randint(arg_keys[3], (FRAMES, SPK), 0, 32768), jax.random.fold_in(arg_keys[3], 1), 0, 32767).astype(jnp.int32)
    band_offset = place_ends(jax.random.randint(arg_keys[4], (FRAMES, SPK), 0, NX - BAND + 1), jax.random.fold_in(arg_keys[4], 1), 0, NX - BAND).astype(jnp.int32)
    owner_map = jax.vmap(lambda own: jax.random.permutation(own, SLAB_VOX))(jax.random.split(arg_keys[5], N_COILS)).reshape((N_COILS, SLAB_VOX)).astype(jnp.int32)
    aif = jnp.clip(jnp.exp(jax.random.uniform(arg_keys[6], (FRAMES,), jnp.float32, math.log(0.2), math.log(5.0))), 0.2, 5.0)
    ktrans = jnp.clip(jnp.exp(math.log(0.4) - 2.9957323 * jax.random.uniform(arg_keys[7], (N_COILS, SLAB_VOX), jnp.float32) ** levels(arg_keys[7], (N_COILS, SLAB_VOX), ((0, 2), (1, 16)), -0.2, 0.2)), 0.02, 0.4)
    kep = jnp.clip(jnp.exp(math.log(2.0) - 2.9957323 * jax.random.uniform(arg_keys[8], (N_COILS, SLAB_VOX), jnp.float32) ** levels(arg_keys[8], (N_COILS, SLAB_VOX), ((0, 2), (1, 16)), -0.2, 0.2)), 0.1, 2.0)
    baseline = jnp.clip(0.5 + 1.5 * jax.random.uniform(arg_keys[9], (2, N_COILS, SLAB_VOX), jnp.float32) ** levels(arg_keys[9], (2, N_COILS, SLAB_VOX), ((1, 2), (2, 16)), -0.2, 0.2), 0.5, 2.0)
    return dict(kspace=kspace, sensitivity=sensitivity, spoke_count=spoke_count, spoke_index=spoke_index, band_offset=band_offset, owner_map=owner_map, aif=aif, ktrans=ktrans, kep=kep, baseline=baseline)


KERNEL = (0.25, 0.75, 0.75, 0.25)
STEP_MINUTES = 0.05
DAMPING = 0.1

def dft_tables(length):
    index = jnp.arange(length, dtype=jnp.int32)
    phase = (index[:, None] * index[None, :] % length).astype(jnp.float32) * (2.0 * math.pi / length)
    norm = 1.0 / math.sqrt(length)
    cosine = (jnp.cos(phase) * norm).astype(jnp.bfloat16)
    sine = (jnp.sin(phase) * norm).astype(jnp.bfloat16)
    column_table = jnp.stack([jnp.stack([cosine, sine], 1), jnp.stack([-sine, cosine], 1)], 0)
    row_table = jnp.stack([jnp.stack([cosine, -sine], 1), jnp.stack([sine, cosine], 1)], 0)
    return (column_table, row_table)

def spoke_weights(count, offset, spoke_number, rows):
    spokes = offset.shape[0]
    row_ids = jnp.arange(rows, dtype=jnp.int32)
    band = jnp.zeros((rows, spokes), jnp.float32)
    for shift_b in range(len(KERNEL)):
        band = band + KERNEL[shift_b] * (row_ids[:, None] == offset[None, :] + shift_b).astype(jnp.float32)
    live = (jnp.arange(spokes, dtype=jnp.int32) < count).astype(jnp.float32)
    turn = (spoke_number * 40503 % 65536).astype(jnp.float32) * (2.0 * math.pi / 65536.0)
    w_cos = band * (live * jnp.cos(turn))[None, :]
    w_sin = band * (live * jnp.sin(turn))[None, :]
    return jnp.stack([jnp.stack([w_cos, -w_sin], 1), jnp.stack([w_sin, w_cos], 1)], 0).astype(jnp.bfloat16)

def aif_matrix(aif):
    length = aif.shape[0]
    index = jnp.arange(length, dtype=jnp.int32)
    lag = index[:, None] - index[None, :]
    table = jnp.take(aif, jnp.clip(lag, 0, length - 1))
    return jnp.where(lag >= 0, table, jnp.zeros_like(table)) * STEP_MINUTES

def tofts_step(images, aif, ktrans, kep, baseline):
    frames = images.shape[0]
    times = jnp.arange(frames, dtype=jnp.int32).astype(jnp.float32) * STEP_MINUTES
    toeplitz = aif_matrix(aif)
    decay = jnp.exp(-times[:, None] * kep[None, :])
    conc = jnp.dot(toeplitz, decay, precision=lax.Precision.HIGHEST)
    slope = jnp.dot(toeplitz, -times[:, None] * decay, precision=lax.Precision.HIGHEST)
    real_part = images[:, 0]
    imag_part = images[:, 1]
    base_r = baseline[0][None, :]
    base_i = baseline[1][None, :]
    scale = 1.0 + ktrans[None, :] * conc
    miss_r = real_part - base_r * scale
    miss_i = imag_part - base_i * scale
    power = baseline[0] * baseline[0] + baseline[1] * baseline[1]
    project = base_r * miss_r + base_i * miss_i
    h_aa = power * lax.optimization_barrier(jnp.sum(conc * conc, 0))
    h_ab = power * ktrans * lax.optimization_barrier(jnp.sum(conc * slope, 0))
    h_bb = power * ktrans * ktrans * lax.optimization_barrier(jnp.sum(slope * slope, 0))
    g_a = lax.optimization_barrier(jnp.sum(conc * project, 0))
    g_b = ktrans * lax.optimization_barrier(jnp.sum(slope * project, 0))
    d_aa = (1.0 + DAMPING) * h_aa + 1.0
    d_bb = (1.0 + DAMPING) * h_bb + 1.0
    determinant = d_aa * d_bb - h_ab * h_ab
    kt_next = ktrans + (d_bb * g_a - h_ab * g_b) / determinant
    kp_next = kep + (d_aa * g_b - h_ab * g_a) / determinant
    conc_next = jnp.dot(toeplitz, jnp.exp(-times[:, None] * kp_next[None, :]), precision=lax.Precision.HIGHEST)
    scale_next = 1.0 + kt_next[None, :] * conc_next
    residual = jnp.stack([real_part - base_r * scale_next, imag_part - base_i * scale_next], 1)
    return (kt_next, kp_next, residual)

def reference(kspace, sensitivity, spoke_count, spoke_index, band_offset, owner_map, aif, ktrans, kep, baseline):
    column_table, row_table = dft_tables(NX)
    sens = sensitivity.astype(jnp.float32)

    def one_frame(pieces):
        frame_data, count, offset, spoke_number = pieces
        weights = spoke_weights(count, offset, spoke_number, NX)
        grid = jnp.einsum('qxps,cpsy->cqxy', weights, frame_data, preferred_element_type=jnp.float32).astype(jnp.bfloat16)
        half = jnp.einsum('cprk,pkqx->cqrx', grid, column_table, preferred_element_type=jnp.float32).astype(jnp.bfloat16)
        coil_image = jnp.einsum('qypr,cprx->cqyx', row_table, half, preferred_element_type=jnp.float32)
        image_r = lax.optimization_barrier(jnp.sum(sens[:, 0] * coil_image[:, 0] + sens[:, 1] * coil_image[:, 1], 0))
        image_i = lax.optimization_barrier(jnp.sum(sens[:, 0] * coil_image[:, 1] - sens[:, 1] * coil_image[:, 0], 0))
        return jnp.stack([image_r, image_i], 0).astype(jnp.bfloat16)
    images = lax.map(one_frame, (kspace, spoke_count, band_offset, spoke_index))
    flat = images.reshape(FRAMES, 2, N_COILS, SLAB_VOX)
    owned = jnp.take_along_axis(flat, owner_map[None, None], axis=3)
    owned = owned.reshape(FRAMES, 2, N_COILS * SLAB_VOX).astype(jnp.float32)
    kt_next, kp_next, residual = tofts_step(owned, aif, ktrans.reshape(-1), kep.reshape(-1), baseline.reshape(2, -1))
    residual = residual.astype(jnp.bfloat16).reshape(FRAMES, 2, N_COILS, SLAB_VOX)
    slab_rows = jnp.arange(N_COILS, dtype=jnp.int32)[:, None]
    placed = jnp.zeros_like(residual).at[:, :, slab_rows, owner_map].set(residual)
    return (kt_next.reshape(N_COILS, SLAB_VOX), kp_next.reshape(N_COILS, SLAB_VOX), placed.reshape(FRAMES, 2, NX, NX))
```

```python
import functools
import math

import jax
import jax.numpy as jnp
import numpy as np
from jax import lax
from jax.experimental import pallas as pl
from jax.experimental.pallas import tpu as pltpu
from jax.sharding import PartitionSpec as P

STEP_MINUTES = 0.05
DAMPING = 0.1
LANES = 128
MESH = pl.DeviceIdType.MESH
F32 = jnp.float32
BF16 = jnp.bfloat16
NT = (((1,), (1,)), ((), ()))


def dft_table(length):
    index = np.arange(length, dtype=np.int64)
    phase = (index[:, None] * index[None, :] % length) * (2.0 * math.pi / length)
    table = np.concatenate([np.cos(phase), np.sin(phase)], 1) / math.sqrt(length)
    return jnp.asarray(table.astype(np.float32)).astype(BF16)


class Chunks:
    def __init__(self, width, voxels):
        self.columns = min(width, voxels)
        self.rows = voxels // self.columns
        self.parts = width // self.columns
        self.height = voxels // LANES

    def pieces(self, number):
        row = number // self.parts * self.rows
        column = number % self.parts * self.columns
        for lane in range(0, self.columns, LANES):
            yield row, slice(column + lane, column + lane + LANES)

    def take(self, plane, number):
        return [plane[row : row + self.rows, lanes] for row, lanes in self.pieces(number)]


def kernel(
    n_frames,
    n_coils,
    kspace,
    sens,
    count,
    spoke_index,
    offset,
    owner,
    aif,
    ktrans,
    kep,
    baseline,
    table,
    kt_out,
    kp_out,
    res_out,
    one_lo,
    spread,
    left,
    right,
    part_send,
    part_recv,
    par_send,
    par_recv,
    img_send,
    img_recv,
    res_send,
    res_recv,
    full,
    part_sems,
    par_sems,
    img_sems,
    res_sems,
):
    _, coils, _, spokes, width = kspace.shape
    slab = owner.shape[1]
    rows = slab // width
    voxels = ktrans.shape[1]
    chunks = Chunks(width, voxels)
    height = chunks.height
    f = lax.axis_index("frames")
    j = lax.axis_index("coils")

    def peer(k):
        return lax.rem(f + k, n_frames)

    def coil_peer(k):
        return lax.rem(j + k, n_coils)

    barrier = pltpu.get_barrier_semaphore()

    def greet(k, _):
        pl.semaphore_signal(
            barrier, inc=1, device_id={"frames": peer(k), "coils": j}, device_id_type=MESH
        )
        return 0

    lax.fori_loop(1, n_frames, greet, 0)
    for k in range(1, n_coils):
        pl.semaphore_signal(
            barrier, inc=1, device_id={"frames": f, "coils": coil_peer(k)}, device_id_type=MESH
        )

    def exchange(send, recv, sems):
        def copy(k):
            to = peer(k)
            return pltpu.make_async_remote_copy(
                src_ref=send.at[to],
                dst_ref=recv.at[f],
                send_sem=sems.at[0, k],
                recv_sem=sems.at[1, k],
                device_id={"frames": to, "coils": j},
                device_id_type=MESH,
            )

        def arrival(k):
            source = lax.rem(f + n_frames - k, n_frames)
            return pltpu.make_async_remote_copy(
                src_ref=send.at[source],
                dst_ref=recv.at[source],
                send_sem=sems.at[0, k],
                recv_sem=sems.at[1, k],
                device_id={"frames": source, "coils": j},
                device_id_type=MESH,
            )

        def start():
            def body(k, _):
                copy(k).start()
                return 0

            lax.fori_loop(1, n_frames, body, 0)
            recv[f] = send[f]

        def wait():
            def body(k, _):
                arrival(k).wait_recv()
                return 0

            lax.fori_loop(1, n_frames, body, 0)

        def drain():
            def body(k, _):
                copy(k).wait_send()
                return 0

            lax.fori_loop(1, n_frames, body, 0)

        return start, wait, drain

    par_start, par_wait, par_drain = exchange(par_send, par_recv, par_sems)
    img_start, img_wait, img_drain = exchange(img_send, img_recv, img_sems)
    res_start, res_wait, res_drain = exchange(res_send, res_recv, res_sems)

    mine = pl.ds(pl.multiple_of(f * voxels, LANES), voxels)
    place = owner[0:1, mine]
    for c in range(1, n_coils):
        place = jnp.where(j == c, owner[c : c + 1, mine], place)
    lo = place & (width - 1)
    hi = lax.shift_right_logical(place, int(math.log2(width)))
    one_lo[...] = jnp.where(
        lax.broadcasted_iota(jnp.int32, (width, voxels), 0) == lo, 1.0, 0.0
    ).astype(BF16)
    in_row = lax.broadcasted_iota(jnp.int32, (rows, voxels), 0) == hi
    values = [ktrans[...], kep[...], baseline[0], baseline[1]]
    for p in range(4):
        spread[p * rows : (p + 1) * rows, :] = jnp.where(in_row, values[p], 0.0).astype(BF16)
    placed = lax.dot_general(spread[...], one_lo[...], NT, preferred_element_type=F32)
    for e in range(n_frames):
        pieces = []
        for p in range(4):
            pieces += chunks.take(placed[p * rows : (p + 1) * rows], e)
        par_send[e] = jnp.concatenate(pieces, 0).astype(BF16)
    pl.semaphore_wait(barrier, n_frames + n_coils - 2)
    par_start()

    number = spoke_index[...]
    turn = ((number * 40503) & 65535).astype(F32) * (2.0 * math.pi / 65536.0)
    live = jnp.where(
        lax.broadcasted_iota(jnp.int32, (1, spokes), 1) < count[0], 1.0, 0.0
    ).astype(F32)
    diagonal = lax.broadcasted_iota(jnp.int32, (spokes, spokes), 0) == (
        lax.broadcasted_iota(jnp.int32, (spokes, spokes), 1)
    )

    def column(row):
        return jnp.sum(jnp.where(diagonal, row, 0.0), 1, keepdims=True)

    w_cos = column(live * jnp.cos(turn))
    w_sin = column(live * jnp.sin(turn))
    first = column(offset[...].astype(F32)).astype(jnp.int32)
    tap = lax.broadcasted_iota(jnp.int32, (spokes, width), 1) - first
    band = jnp.where(
        (tap == 0) | (tap == 3), 0.25, jnp.where((tap == 1) | (tap == 2), 0.75, 0.0)
    )
    m_cos = band * w_cos
    m_sin = band * w_sin
    m_a = jnp.concatenate([m_cos, m_sin], 0).astype(BF16)
    m_b = jnp.concatenate([-m_sin, m_cos], 0).astype(BF16)
    left[...] = (
        lax.dot_general(table[:, :width], m_a, NT, preferred_element_type=F32)
        + lax.dot_general(table[:, width:], m_b, NT, preferred_element_type=F32)
    ).astype(BF16)

    lines = jnp.dot(
        kspace[0].reshape(coils * 2 * spokes, width), table[...], preferred_element_type=F32
    )
    for c in range(coils):
        real = lines[2 * c * spokes : (2 * c + 1) * spokes]
        imag = lines[(2 * c + 1) * spokes : (2 * c + 2) * spokes]
        h_r = (real[:, :width] - imag[:, width:]).astype(BF16)
        h_i = (real[:, width:] + imag[:, :width]).astype(BF16)
        at = 2 * c * width
        right[:spokes, at : at + width] = h_r
        right[:spokes, at + width : at + 2 * width] = h_i
        right[spokes:, at : at + width] = -h_i
        right[spokes:, at + width : at + 2 * width] = h_r

    def partial(which):
        top = pl.multiple_of(which * rows, rows)
        coil_image = jnp.dot(
            left[pl.ds(top, rows), :], right[...], preferred_element_type=F32
        )
        image_r = jnp.zeros((rows, width), F32)
        image_i = jnp.zeros((rows, width), F32)
        for c in range(coils):
            s_r = sens[c, 0, pl.ds(top, rows), :].astype(F32)
            s_i = sens[c, 1, pl.ds(top, rows), :].astype(F32)
            c_r = coil_image[:, 2 * c * width : (2 * c + 1) * width]
            c_i = coil_image[:, (2 * c + 1) * width : (2 * c + 2) * width]
            image_r = image_r + s_r * c_r + s_i * c_i
            image_i = image_i + s_r * c_i - s_i * c_r
        return image_r, image_i

    def part_copy(k):
        return pltpu.make_async_remote_copy(
            src_ref=part_send.at[k - 1],
            dst_ref=part_recv.at[k - 1],
            send_sem=part_sems.at[0, k],
            recv_sem=part_sems.at[1, k],
            device_id={"frames": f, "coils": coil_peer(k)},
            device_id_type=MESH,
        )

    for k in range(1, n_coils):
        image_r, image_i = partial(coil_peer(k))
        part_send[k - 1, 0] = image_r
        part_send[k - 1, 1] = image_i
        part_copy(k).start()
    image_r, image_i = partial(j)
    for k in range(1, n_coils):
        part_copy(k).wait_recv()
        image_r = image_r + part_recv[k - 1, 0]
        image_i = image_i + part_recv[k - 1, 1]
    for e in range(n_frames):
        pieces = chunks.take(image_r, e) + chunks.take(image_i, e)
        img_send[e] = jnp.concatenate(pieces, 0).astype(BF16)
    img_start()

    par_wait()
    params = par_recv[0].astype(F32)
    for e in range(1, n_frames):
        params = params + par_recv[e].astype(F32)
    kt, kp, base_r, base_i = [params[p * height : (p + 1) * height] for p in range(4)]
    taps = [aif[t] * STEP_MINUTES for t in range(n_frames)]
    decay = [jnp.exp(-(t * STEP_MINUTES) * kp) for t in range(n_frames)]
    drift = [decay[t] * -(t * STEP_MINUTES) for t in range(n_frames)]

    def convolve(curve, t):
        total = taps[t] * curve[0]
        for m in range(1, t + 1):
            total = total + taps[t - m] * curve[m]
        return total

    conc = [convolve(decay, t) for t in range(n_frames)]
    slope = [convolve(drift, t) for t in range(n_frames)]
    power = base_r * base_r + base_i * base_i
    h_aa = power * sum(c * c for c in conc)
    h_ab = power * kt * sum(c * s for c, s in zip(conc, slope))
    h_bb = power * kt * kt * sum(s * s for s in slope)
    d_aa = (1.0 + DAMPING) * h_aa + 1.0
    d_bb = (1.0 + DAMPING) * h_bb + 1.0
    determinant = d_aa * d_bb - h_ab * h_ab

    img_wait()
    g_a = jnp.zeros_like(kt)
    g_b = jnp.zeros_like(kt)
    for t in range(n_frames):
        image = img_recv[t].astype(F32)
        scale = 1.0 + kt * conc[t]
        project = base_r * (image[:height] - base_r * scale) + base_i * (
            image[height:] - base_i * scale
        )
        g_a = g_a + conc[t] * project
        g_b = g_b + slope[t] * project
    g_b = kt * g_b
    step_kt = (d_bb * g_a - h_ab * g_b) / determinant
    step_kp = (d_aa * g_b - h_ab * g_a) / determinant
    kt_next = kt + step_kt
    kp_next = kp + step_kp
    decay = [jnp.exp(-(t * STEP_MINUTES) * kp_next) for t in range(n_frames)]
    for t in range(n_frames):
        image = img_recv[t].astype(F32)
        scale = 1.0 + kt_next * convolve(decay, t)
        res_send[t] = jnp.concatenate(
            [image[:height] - base_r * scale, image[height:] - base_i * scale, step_kt, step_kp], 0
        ).astype(BF16)
    res_start()

    res_wait()
    for e in range(n_frames):
        block = res_recv[e].astype(F32)
        at = 0
        for p in range(4):
            for row, lanes in chunks.pieces(e):
                full[p * rows + row : p * rows + row + chunks.rows, lanes] = block[
                    at : at + chunks.rows
                ]
                at += chunks.rows
    for p in range(2):
        res_out[0, p] = full[p * rows : (p + 1) * rows, :].astype(BF16)
    picked = jnp.dot(
        full[2 * rows :, :].astype(BF16), one_lo[...], preferred_element_type=F32
    )
    in_row = lax.broadcasted_iota(jnp.int32, (rows, voxels), 0) == hi
    kt_out[...] = ktrans[...] + jnp.sum(
        jnp.where(in_row, picked[:rows], 0.0), 0, keepdims=True
    )
    kp_out[...] = kep[...] + jnp.sum(
        jnp.where(in_row, picked[rows:], 0.0), 0, keepdims=True
    )
    for k in range(1, n_coils):
        part_copy(k).wait_send()
    par_drain()
    img_drain()
    res_drain()


def shards(
    kspace,
    sensitivity,
    spoke_count,
    spoke_index,
    band_offset,
    owner_map,
    aif,
    ktrans,
    kep,
    baseline,
):
    n_frames = lax.axis_size("frames")
    n_coils = lax.axis_size("coils")
    _, coils, _, spokes, width = kspace.shape
    voxels = ktrans.shape[1]
    rows = owner_map.shape[1] // width
    height = voxels // LANES
    vmem = pl.BlockSpec(memory_space=pltpu.VMEM)
    smem = pl.BlockSpec(memory_space=pltpu.SMEM)
    pair = pltpu.SemaphoreType.DMA((2, n_frames))
    return pl.pallas_call(
        functools.partial(kernel, n_frames, n_coils),
        out_shape=[
            jax.ShapeDtypeStruct((1, voxels), F32),
            jax.ShapeDtypeStruct((1, voxels), F32),
            jax.ShapeDtypeStruct((1, 2, rows, width), BF16),
        ],
        in_specs=[vmem, vmem, smem, vmem, vmem, vmem, smem, vmem, vmem, vmem, vmem],
        out_specs=[vmem, vmem, vmem],
        scratch_shapes=[
            pltpu.VMEM((width, voxels), BF16),
            pltpu.VMEM((4 * rows, voxels), BF16),
            pltpu.VMEM((width, 2 * spokes), BF16),
            pltpu.VMEM((2 * spokes, coils * 2 * width), BF16),
            pltpu.VMEM((n_coils - 1, 2, rows, width), F32),
            pltpu.VMEM((n_coils - 1, 2, rows, width), F32),
            pltpu.VMEM((n_frames, 4 * height, LANES), BF16),
            pltpu.VMEM((n_frames, 4 * height, LANES), BF16),
            pltpu.VMEM((n_frames, 2 * height, LANES), BF16),
            pltpu.VMEM((n_frames, 2 * height, LANES), BF16),
            pltpu.VMEM((n_frames, 4 * height, LANES), BF16),
            pltpu.VMEM((n_frames, 4 * height, LANES), BF16),
            pltpu.VMEM((4 * rows, width), F32),
            pltpu.SemaphoreType.DMA((2, n_coils)),
            pair,
            pair,
            pair,
        ],
        compiler_params=pltpu.CompilerParams(
            collective_id=0, has_side_effects=True, vmem_limit_bytes=48 * 1024 * 1024
        ),
    )(
        kspace,
        sensitivity,
        spoke_count,
        spoke_index,
        band_offset,
        owner_map,
        aif,
        ktrans,
        kep,
        baseline.reshape(2, 1, voxels),
        dft_table(width),
    )


def solution(mesh):
    in_specs = (
        P("frames", "coils", None, None, None),
        P("coils", None, None, None),
        P("frames"),
        P("frames", None),
        P("frames", None),
        P(),
        P(),
        P("coils", "frames"),
        P("coils", "frames"),
        P(None, "coils", "frames"),
    )
    out_specs = (P("coils", "frames"), P("coils", "frames"), P("frames", None, "coils", None))
    return jax.shard_map(shards, mesh=mesh, in_specs=in_specs, out_specs=out_specs, check_vma=False)
```

```python
import functools
import math

import jax
import jax.numpy as jnp
import numpy as np
from jax import lax
from jax.experimental import pallas as pl
from jax.experimental.pallas import tpu as pltpu
from jax.sharding import PartitionSpec as P

STEP_MINUTES = 0.05
DAMPING = 0.1
LANES = 128
MESH = pl.DeviceIdType.MESH
F32 = jnp.float32
BF16 = jnp.bfloat16
NT = (((1,), (1,)), ((), ()))


def dft_table(length):
    index = np.arange(length, dtype=np.int64)
    phase = (index[:, None] * index[None, :] % length) * (2.0 * math.pi / length)
    table = np.concatenate([np.cos(phase), np.sin(phase)], 1) / math.sqrt(length)
    return jnp.asarray(table.astype(np.float32)).astype(BF16)


class Chunks:
    def __init__(self, width, voxels):
        self.columns = min(width, voxels)
        self.rows = voxels // self.columns
        self.parts = width // self.columns
        self.height = voxels // LANES

    def pieces(self, number):
        row = number // self.parts * self.rows
        column = number % self.parts * self.columns
        for lane in range(0, self.columns, LANES):
            yield row, slice(column + lane, column + lane + LANES)

    def take(self, plane, number):
        return [plane[row : row + self.rows, lanes] for row, lanes in self.pieces(number)]


def kernel(
    n_frames,
    n_coils,
    kspace_in,
    sens_in,
    count_in,
    spoke_index_in,
    offset_in,
    owner_in,
    aif_in,
    ktrans_in,
    kep_in,
    baseline_in,
    table_in,
    kt_out,
    kp_out,
    res_out,
    kspace,
    sens,
    count,
    spoke_index,
    offset,
    owner,
    aif,
    ktrans,
    kep,
    baseline,
    table,
    input_sems,
    one_lo,
    spread,
    left,
    right,
    part_send,
    part_recv,
    par_send,
    par_recv,
    img_send,
    img_recv,
    res_send,
    res_recv,
    full,
    part_sems,
    par_sems,
    img_sems,
    res_sems,
):
    _, coils, _, spokes, width = kspace.shape
    rows = owner_in.shape[1] // width
    voxels = ktrans.shape[1]
    chunks = Chunks(width, voxels)
    height = chunks.height
    f = lax.axis_index("frames")
    j = lax.axis_index("coils")
    mine = pl.ds(pl.multiple_of(f * voxels, LANES), voxels)
    loads = {}
    for name, source, target in (
        ("owner", owner_in.at[:, mine], owner),
        ("ktrans", ktrans_in, ktrans),
        ("kep", kep_in, kep),
        ("baseline", baseline_in, baseline),
        ("table", table_in, table),
        ("index", spoke_index_in, spoke_index),
        ("offset", offset_in, offset),
        ("count", count_in, count),
        ("kspace", kspace_in, kspace),
        ("sens", sens_in, sens),
        ("aif", aif_in, aif),
    ):
        loads[name] = pltpu.make_async_copy(source, target, input_sems.at[len(loads)])
        loads[name].start()

    def loaded(*names):
        for name in names:
            loads[name].wait()

    def peer(k):
        return lax.rem(f + k, n_frames)

    def coil_peer(k):
        return lax.rem(j + k, n_coils)

    barrier = pltpu.get_barrier_semaphore()

    def greet(k, _):
        pl.semaphore_signal(
            barrier, inc=1, device_id={"frames": peer(k), "coils": j}, device_id_type=MESH
        )
        return 0

    lax.fori_loop(1, n_frames, greet, 0)
    for k in range(1, n_coils):
        pl.semaphore_signal(
            barrier, inc=1, device_id={"frames": f, "coils": coil_peer(k)}, device_id_type=MESH
        )

    def exchange(send, recv, sems):
        def copy(k):
            to = peer(k)
            return pltpu.make_async_remote_copy(
                src_ref=send.at[to],
                dst_ref=recv.at[f],
                send_sem=sems.at[0, k],
                recv_sem=sems.at[1, k],
                device_id={"frames": to, "coils": j},
                device_id_type=MESH,
            )

        def arrival(k):
            source = lax.rem(f + n_frames - k, n_frames)
            return pltpu.make_async_remote_copy(
                src_ref=send.at[source],
                dst_ref=recv.at[source],
                send_sem=sems.at[0, k],
                recv_sem=sems.at[1, k],
                device_id={"frames": source, "coils": j},
                device_id_type=MESH,
            )

        def start():
            def body(k, _):
                copy(k).start()
                return 0

            lax.fori_loop(1, n_frames, body, 0)
            recv[f] = send[f]

        def wait():
            def body(k, _):
                arrival(k).wait_recv()
                return 0

            lax.fori_loop(1, n_frames, body, 0)

        def drain():
            def body(k, _):
                copy(k).wait_send()
                return 0

            lax.fori_loop(1, n_frames, body, 0)

        return start, wait, drain

    par_start, par_wait, par_drain = exchange(par_send, par_recv, par_sems)
    img_start, img_wait, img_drain = exchange(img_send, img_recv, img_sems)
    res_start, res_wait, res_drain = exchange(res_send, res_recv, res_sems)

    loaded("owner", "ktrans", "kep", "baseline")
    place = owner[0:1, :]
    for c in range(1, n_coils):
        place = jnp.where(j == c, owner[c : c + 1, :], place)
    lo = place & (width - 1)
    hi = lax.shift_right_logical(place, int(math.log2(width)))
    one_lo[...] = jnp.where(
        lax.broadcasted_iota(jnp.int32, (width, voxels), 0) == lo, 1.0, 0.0
    ).astype(BF16)
    in_row = lax.broadcasted_iota(jnp.int32, (rows, voxels), 0) == hi
    values = [ktrans[...], kep[...], baseline[0], baseline[1]]
    for p in range(4):
        spread[p * rows : (p + 1) * rows, :] = jnp.where(in_row, values[p], 0.0).astype(BF16)
    placed = lax.dot_general(spread[...], one_lo[...], NT, preferred_element_type=F32)
    for e in range(n_frames):
        pieces = []
        for p in range(4):
            pieces += chunks.take(placed[p * rows : (p + 1) * rows], e)
        par_send[e] = jnp.concatenate(pieces, 0).astype(BF16)
    pl.semaphore_wait(barrier, n_frames + n_coils - 2)
    par_start()

    loaded("index", "offset", "count", "table")
    number = spoke_index[...]
    turn = ((number * 40503) & 65535).astype(F32) * (2.0 * math.pi / 65536.0)
    live = jnp.where(
        lax.broadcasted_iota(jnp.int32, (1, spokes), 1) < count[0], 1.0, 0.0
    ).astype(F32)
    diagonal = lax.broadcasted_iota(jnp.int32, (spokes, spokes), 0) == (
        lax.broadcasted_iota(jnp.int32, (spokes, spokes), 1)
    )

    def column(row):
        return jnp.sum(jnp.where(diagonal, row, 0.0), 1, keepdims=True)

    w_cos = column(live * jnp.cos(turn))
    w_sin = column(live * jnp.sin(turn))
    first = column(offset[...].astype(F32)).astype(jnp.int32)
    tap = lax.broadcasted_iota(jnp.int32, (spokes, width), 1) - first
    band = jnp.where(
        (tap == 0) | (tap == 3), 0.25, jnp.where((tap == 1) | (tap == 2), 0.75, 0.0)
    )
    m_cos = band * w_cos
    m_sin = band * w_sin
    m_a = jnp.concatenate([m_cos, m_sin], 0).astype(BF16)
    m_b = jnp.concatenate([-m_sin, m_cos], 0).astype(BF16)
    left[...] = (
        lax.dot_general(table[:, :width], m_a, NT, preferred_element_type=F32)
        + lax.dot_general(table[:, width:], m_b, NT, preferred_element_type=F32)
    ).astype(BF16)

    loaded("kspace")
    lines = jnp.dot(
        kspace[0].reshape(coils * 2 * spokes, width), table[...], preferred_element_type=F32
    )
    for c in range(coils):
        real = lines[2 * c * spokes : (2 * c + 1) * spokes]
        imag = lines[(2 * c + 1) * spokes : (2 * c + 2) * spokes]
        h_r = (real[:, :width] - imag[:, width:]).astype(BF16)
        h_i = (real[:, width:] + imag[:, :width]).astype(BF16)
        at = 2 * c * width
        right[:spokes, at : at + width] = h_r
        right[:spokes, at + width : at + 2 * width] = h_i
        right[spokes:, at : at + width] = -h_i
        right[spokes:, at + width : at + 2 * width] = h_r

    def partial(which):
        top = pl.multiple_of(which * rows, rows)
        coil_image = jnp.dot(
            left[pl.ds(top, rows), :], right[...], preferred_element_type=F32
        )
        image_r = jnp.zeros((rows, width), F32)
        image_i = jnp.zeros((rows, width), F32)
        for c in range(coils):
            s_r = sens[c, 0, pl.ds(top, rows), :].astype(F32)
            s_i = sens[c, 1, pl.ds(top, rows), :].astype(F32)
            c_r = coil_image[:, 2 * c * width : (2 * c + 1) * width]
            c_i = coil_image[:, (2 * c + 1) * width : (2 * c + 2) * width]
            image_r = image_r + s_r * c_r + s_i * c_i
            image_i = image_i + s_r * c_i - s_i * c_r
        return image_r, image_i

    loaded("sens")

    def part_copy(k):
        return pltpu.make_async_remote_copy(
            src_ref=part_send.at[k - 1],
            dst_ref=part_recv.at[k - 1],
            send_sem=part_sems.at[0, k],
            recv_sem=part_sems.at[1, k],
            device_id={"frames": f, "coils": coil_peer(k)},
            device_id_type=MESH,
        )

    for k in range(1, n_coils):
        image_r, image_i = partial(coil_peer(k))
        part_send[k - 1, 0] = image_r
        part_send[k - 1, 1] = image_i
        part_copy(k).start()
    image_r, image_i = partial(j)
    for k in range(1, n_coils):
        part_copy(k).wait_recv()
        image_r = image_r + part_recv[k - 1, 0]
        image_i = image_i + part_recv[k - 1, 1]
    for e in range(n_frames):
        pieces = chunks.take(image_r, e) + chunks.take(image_i, e)
        img_send[e] = jnp.concatenate(pieces, 0).astype(BF16)
    img_start()

    par_wait()
    params = par_recv[0].astype(F32)
    for e in range(1, n_frames):
        params = params + par_recv[e].astype(F32)
    kt, kp, base_r, base_i = [params[p * height : (p + 1) * height] for p in range(4)]
    loaded("aif")
    taps = [aif[t] * STEP_MINUTES for t in range(n_frames)]
    decay = [jnp.exp(-(t * STEP_MINUTES) * kp) for t in range(n_frames)]
    drift = [decay[t] * -(t * STEP_MINUTES) for t in range(n_frames)]

    def convolve(curve, t):
        total = taps[t] * curve[0]
        for m in range(1, t + 1):
            total = total + taps[t - m] * curve[m]
        return total

    conc = [convolve(decay, t) for t in range(n_frames)]
    slope = [convolve(drift, t) for t in range(n_frames)]
    power = base_r * base_r + base_i * base_i
    h_aa = power * sum(c * c for c in conc)
    h_ab = power * kt * sum(c * s for c, s in zip(conc, slope))
    h_bb = power * kt * kt * sum(s * s for s in slope)
    d_aa = (1.0 + DAMPING) * h_aa + 1.0
    d_bb = (1.0 + DAMPING) * h_bb + 1.0
    determinant = d_aa * d_bb - h_ab * h_ab

    img_wait()
    g_a = jnp.zeros_like(kt)
    g_b = jnp.zeros_like(kt)
    for t in range(n_frames):
        image = img_recv[t].astype(F32)
        scale = 1.0 + kt * conc[t]
        project = base_r * (image[:height] - base_r * scale) + base_i * (
            image[height:] - base_i * scale
        )
        g_a = g_a + conc[t] * project
        g_b = g_b + slope[t] * project
    g_b = kt * g_b
    step_kt = (d_bb * g_a - h_ab * g_b) / determinant
    step_kp = (d_aa * g_b - h_ab * g_a) / determinant
    kt_next = kt + step_kt
    kp_next = kp + step_kp
    decay = [jnp.exp(-(t * STEP_MINUTES) * kp_next) for t in range(n_frames)]
    for t in range(n_frames):
        image = img_recv[t].astype(F32)
        scale = 1.0 + kt_next * convolve(decay, t)
        res_send[t] = jnp.concatenate(
            [image[:height] - base_r * scale, image[height:] - base_i * scale, step_kt, step_kp], 0
        ).astype(BF16)
    res_start()

    res_wait()
    for e in range(n_frames):
        block = res_recv[e].astype(F32)
        at = 0
        for p in range(4):
            for row, lanes in chunks.pieces(e):
                full[p * rows + row : p * rows + row + chunks.rows, lanes] = block[
                    at : at + chunks.rows
                ]
                at += chunks.rows
    for p in range(2):
        res_out[0, p] = full[p * rows : (p + 1) * rows, :].astype(BF16)
    picked = jnp.dot(
        full[2 * rows :, :].astype(BF16), one_lo[...], preferred_element_type=F32
    )
    in_row = lax.broadcasted_iota(jnp.int32, (rows, voxels), 0) == hi
    kt_out[...] = ktrans[...] + jnp.sum(
        jnp.where(in_row, picked[:rows], 0.0), 0, keepdims=True
    )
    kp_out[...] = kep[...] + jnp.sum(
        jnp.where(in_row, picked[rows:], 0.0), 0, keepdims=True
    )
    for k in range(1, n_coils):
        part_copy(k).wait_send()
    par_drain()
    img_drain()
    res_drain()


def shards(
    kspace,
    sensitivity,
    spoke_count,
    spoke_index,
    band_offset,
    owner_map,
    aif,
    ktrans,
    kep,
    baseline,
):
    n_frames = lax.axis_size("frames")
    n_coils = lax.axis_size("coils")
    _, coils, _, spokes, width = kspace.shape
    voxels = ktrans.shape[1]
    rows = owner_map.shape[1] // width
    height = voxels // LANES
    vmem = pl.BlockSpec(memory_space=pltpu.VMEM)
    hbm = pl.BlockSpec(memory_space=pltpu.HBM)
    operands = (
        kspace,
        sensitivity,
        spoke_count,
        spoke_index,
        band_offset,
        owner_map,
        aif,
        ktrans,
        kep,
        baseline.reshape(2, 1, voxels),
        dft_table(width),
    )
    landing = [
        (pltpu.SMEM if x.ndim == 1 else pltpu.VMEM)(x.shape, x.dtype) for x in operands
    ]
    landing[5] = pltpu.VMEM((n_coils, voxels), jnp.int32)
    pair = pltpu.SemaphoreType.DMA((2, n_frames))
    return pl.pallas_call(
        functools.partial(kernel, n_frames, n_coils),
        out_shape=[
            jax.ShapeDtypeStruct((1, voxels), F32),
            jax.ShapeDtypeStruct((1, voxels), F32),
            jax.ShapeDtypeStruct((1, 2, rows, width), BF16),
        ],
        in_specs=[hbm] * len(operands),
        out_specs=[vmem, vmem, vmem],
        scratch_shapes=landing
        + [
            pltpu.SemaphoreType.DMA((len(operands),)),
            pltpu.VMEM((width, voxels), BF16),
            pltpu.VMEM((4 * rows, voxels), BF16),
            pltpu.VMEM((width, 2 * spokes), BF16),
            pltpu.VMEM((2 * spokes, coils * 2 * width), BF16),
            pltpu.VMEM((n_coils - 1, 2, rows, width), F32),
            pltpu.VMEM((n_coils - 1, 2, rows, width), F32),
            pltpu.VMEM((n_frames, 4 * height, LANES), BF16),
            pltpu.VMEM((n_frames, 4 * height, LANES), BF16),
            pltpu.VMEM((n_frames, 2 * height, LANES), BF16),
            pltpu.VMEM((n_frames, 2 * height, LANES), BF16),
            pltpu.VMEM((n_frames, 4 * height, LANES), BF16),
            pltpu.VMEM((n_frames, 4 * height, LANES), BF16),
            pltpu.VMEM((4 * rows, width), F32),
            pltpu.SemaphoreType.DMA((2, n_coils)),
            pair,
            pair,
            pair,
        ],
        compiler_params=pltpu.CompilerParams(
            collective_id=0, has_side_effects=True, vmem_limit_bytes=56 * 1024 * 1024
        ),
    )(*operands)


def solution(mesh):
    in_specs = (
        P("frames", "coils", None, None, None),
        P("coils", None, None, None),
        P("frames"),
        P("frames", None),
        P("frames", None),
        P(),
        P(),
        P("coils", "frames"),
        P("coils", "frames"),
        P(None, "coils", "frames"),
    )
    out_specs = (P("coils", "frames"), P("coils", "frames"), P("frames", None, "coils", None))
    return jax.shard_map(shards, mesh=mesh, in_specs=in_specs, out_specs=out_specs, check_vma=False)
```

```python
import functools
import math

import jax
import jax.numpy as jnp
import numpy as np
from jax import lax
from jax.experimental import pallas as pl
from jax.experimental.pallas import tpu as pltpu
from jax.sharding import PartitionSpec as P

STEP_MINUTES = 0.05
DAMPING = 0.1
LANES = 128
MESH = pl.DeviceIdType.MESH
F32 = jnp.float32
BF16 = jnp.bfloat16
NT = (((1,), (1,)), ((), ()))


def dft_table(length):
    index = np.arange(length, dtype=np.int64)
    phase = (index[:, None] * index[None, :] % length) * (2.0 * math.pi / length)
    table = np.concatenate([np.cos(phase), np.sin(phase)], 1) / math.sqrt(length)
    return jnp.asarray(table.astype(np.float32)).astype(BF16)


class Chunks:
    def __init__(self, width, voxels):
        self.columns = min(width, voxels)
        self.rows = voxels // self.columns
        self.parts = width // self.columns
        self.height = voxels // LANES

    def pieces(self, number):
        row = number // self.parts * self.rows
        column = number % self.parts * self.columns
        for lane in range(0, self.columns, LANES):
            yield row, slice(column + lane, column + lane + LANES)

    def take(self, plane, number):
        return [plane[row : row + self.rows, lanes] for row, lanes in self.pieces(number)]


def kernel(
    n_frames,
    n_coils,
    kspace_in,
    sens_in,
    count_in,
    spoke_index_in,
    offset_in,
    owner_in,
    aif_in,
    ktrans_in,
    kep_in,
    baseline_in,
    table_in,
    kt_out,
    kp_out,
    res_out,
    kspace,
    sens,
    count,
    spoke_index,
    offset,
    owner,
    aif,
    ktrans,
    kep,
    baseline,
    table,
    input_sems,
    one_lo,
    spread,
    left,
    right,
    part_send,
    part_recv,
    par_send,
    par_recv,
    img_send,
    img_recv,
    res_send,
    res_recv,
    full,
    part_sems,
    par_sems,
    img_sems,
    res_sems,
):
    _, coils, _, spokes, width = kspace.shape
    rows = owner_in.shape[1] // width
    voxels = ktrans.shape[1]
    chunks = Chunks(width, voxels)
    height = chunks.height
    f = lax.axis_index("frames")
    j = lax.axis_index("coils")
    mine = pl.ds(pl.multiple_of(f * voxels, LANES), voxels)
    loads = {}
    for name, source, target in (
        ("owner", owner_in.at[:, mine], owner),
        ("ktrans", ktrans_in, ktrans),
        ("kep", kep_in, kep),
        ("baseline", baseline_in, baseline),
        ("table", table_in, table),
        ("index", spoke_index_in, spoke_index),
        ("offset", offset_in, offset),
        ("count", count_in, count),
        ("kspace", kspace_in, kspace),
        ("sens", sens_in, sens),
        ("aif", aif_in, aif),
    ):
        loads[name] = pltpu.make_async_copy(source, target, input_sems.at[len(loads)])
        loads[name].start()

    def loaded(*names):
        for name in names:
            loads[name].wait()

    def peer(k):
        return lax.rem(f + k, n_frames)

    def coil_peer(k):
        return lax.rem(j + k, n_coils)

    barrier = pltpu.get_barrier_semaphore()

    def greet(k, _):
        pl.semaphore_signal(
            barrier, inc=1, device_id={"frames": peer(k), "coils": j}, device_id_type=MESH
        )
        return 0

    lax.fori_loop(1, n_frames, greet, 0)
    for k in range(1, n_coils):
        pl.semaphore_signal(
            barrier, inc=1, device_id={"frames": f, "coils": coil_peer(k)}, device_id_type=MESH
        )

    def exchange(send, recv, sems):
        def copy(k):
            to = peer(k)
            return pltpu.make_async_remote_copy(
                src_ref=send.at[to],
                dst_ref=recv.at[f],
                send_sem=sems.at[0, k],
                recv_sem=sems.at[1, k],
                device_id={"frames": to, "coils": j},
                device_id_type=MESH,
            )

        def arrival(k):
            source = lax.rem(f + n_frames - k, n_frames)
            return pltpu.make_async_remote_copy(
                src_ref=send.at[source],
                dst_ref=recv.at[source],
                send_sem=sems.at[0, k],
                recv_sem=sems.at[1, k],
                device_id={"frames": source, "coils": j},
                device_id_type=MESH,
            )

        def start():
            def body(k, _):
                copy(k).start()
                return 0

            lax.fori_loop(1, n_frames, body, 0)
            recv[f] = send[f]

        def wait():
            def body(k, _):
                arrival(k).wait_recv()
                return 0

            lax.fori_loop(1, n_frames, body, 0)

        def drain():
            def body(k, _):
                copy(k).wait_send()
                return 0

            lax.fori_loop(1, n_frames, body, 0)

        return start, wait, drain

    par_start, par_wait, par_drain = exchange(par_send, par_recv, par_sems)
    img_start, img_wait, img_drain = exchange(img_send, img_recv, img_sems)
    res_start, res_wait, res_drain = exchange(res_send, res_recv, res_sems)

    loaded("owner", "ktrans", "kep", "baseline")
    place = owner[0:1, :]
    for c in range(1, n_coils):
        place = jnp.where(j == c, owner[c : c + 1, :], place)
    lo = place & (width - 1)
    hi = lax.shift_right_logical(place, int(math.log2(width)))
    one_lo[...] = jnp.where(
        lax.broadcasted_iota(jnp.int32, (width, voxels), 0) == lo, 1.0, 0.0
    ).astype(BF16)
    in_row = lax.broadcasted_iota(jnp.int32, (rows, voxels), 0) == hi
    values = [ktrans[...], kep[...], baseline[0], baseline[1]]
    for p in range(4):
        spread[p * rows : (p + 1) * rows, :] = jnp.where(in_row, values[p], 0.0).astype(BF16)
    placed = lax.dot_general(spread[...], one_lo[...], NT, preferred_element_type=F32)
    for e in range(n_frames):
        pieces = []
        for p in range(4):
            pieces += chunks.take(placed[p * rows : (p + 1) * rows], e)
        par_send[e] = jnp.concatenate(pieces, 0).astype(BF16)

    loaded("index", "offset", "count", "table")
    number = spoke_index[...]
    turn = ((number * 40503) & 65535).astype(F32) * (2.0 * math.pi / 65536.0)
    live = jnp.where(
        lax.broadcasted_iota(jnp.int32, (1, spokes), 1) < count[0], 1.0, 0.0
    ).astype(F32)
    diagonal = lax.broadcasted_iota(jnp.int32, (spokes, spokes), 0) == (
        lax.broadcasted_iota(jnp.int32, (spokes, spokes), 1)
    )

    def column(row):
        return jnp.sum(jnp.where(diagonal, row, 0.0), 1, keepdims=True)

    w_cos = column(live * jnp.cos(turn))
    w_sin = column(live * jnp.sin(turn))
    first = column(offset[...].astype(F32)).astype(jnp.int32)
    tap = lax.broadcasted_iota(jnp.int32, (spokes, width), 1) - first
    band = jnp.where(
        (tap == 0) | (tap == 3), 0.25, jnp.where((tap == 1) | (tap == 2), 0.75, 0.0)
    )
    m_cos = band * w_cos
    m_sin = band * w_sin
    m_a = jnp.concatenate([m_cos, m_sin], 0).astype(BF16)
    m_b = jnp.concatenate([-m_sin, m_cos], 0).astype(BF16)
    left[...] = (
        lax.dot_general(table[:, :width], m_a, NT, preferred_element_type=F32)
        + lax.dot_general(table[:, width:], m_b, NT, preferred_element_type=F32)
    ).astype(BF16)

    loaded("kspace")
    lines = jnp.dot(
        kspace[0].reshape(coils * 2 * spokes, width), table[...], preferred_element_type=F32
    )
    for c in range(coils):
        real = lines[2 * c * spokes : (2 * c + 1) * spokes]
        imag = lines[(2 * c + 1) * spokes : (2 * c + 2) * spokes]
        h_r = (real[:, :width] - imag[:, width:]).astype(BF16)
        h_i = (real[:, width:] + imag[:, :width]).astype(BF16)
        at = 2 * c * width
        right[:spokes, at : at + width] = h_r
        right[:spokes, at + width : at + 2 * width] = h_i
        right[spokes:, at : at + width] = -h_i
        right[spokes:, at + width : at + 2 * width] = h_r

    def partial(which):
        top = pl.multiple_of(which * rows, rows)
        coil_image = jnp.dot(
            left[pl.ds(top, rows), :], right[...], preferred_element_type=F32
        )
        image_r = jnp.zeros((rows, width), F32)
        image_i = jnp.zeros((rows, width), F32)
        for c in range(coils):
            s_r = sens[c, 0, pl.ds(top, rows), :].astype(F32)
            s_i = sens[c, 1, pl.ds(top, rows), :].astype(F32)
            c_r = coil_image[:, 2 * c * width : (2 * c + 1) * width]
            c_i = coil_image[:, (2 * c + 1) * width : (2 * c + 2) * width]
            image_r = image_r + s_r * c_r + s_i * c_i
            image_i = image_i + s_r * c_i - s_i * c_r
        return image_r, image_i

    loaded("sens")

    def part_copy(k):
        return pltpu.make_async_remote_copy(
            src_ref=part_send.at[k - 1],
            dst_ref=part_recv.at[k - 1],
            send_sem=part_sems.at[0, k],
            recv_sem=part_sems.at[1, k],
            device_id={"frames": f, "coils": coil_peer(k)},
            device_id_type=MESH,
        )

    for k in range(1, n_coils):
        image_r, image_i = partial(coil_peer(k))
        part_send[k - 1, 0] = image_r
        part_send[k - 1, 1] = image_i
    pl.semaphore_wait(barrier, n_frames + n_coils - 2)
    for k in range(1, n_coils):
        part_copy(k).start()
    par_start()
    image_r, image_i = partial(j)
    for k in range(1, n_coils):
        part_copy(k).wait_recv()
        image_r = image_r + part_recv[k - 1, 0]
        image_i = image_i + part_recv[k - 1, 1]
    for e in range(n_frames):
        pieces = chunks.take(image_r, e) + chunks.take(image_i, e)
        img_send[e] = jnp.concatenate(pieces, 0).astype(BF16)
    img_start()

    par_wait()
    params = par_recv[0].astype(F32)
    for e in range(1, n_frames):
        params = params + par_recv[e].astype(F32)
    kt, kp, base_r, base_i = [params[p * height : (p + 1) * height] for p in range(4)]
    loaded("aif")
    taps = [aif[t] * STEP_MINUTES for t in range(n_frames)]
    decay = [jnp.exp(-(t * STEP_MINUTES) * kp) for t in range(n_frames)]
    drift = [decay[t] * -(t * STEP_MINUTES) for t in range(n_frames)]

    def convolve(curve, t):
        total = taps[t] * curve[0]
        for m in range(1, t + 1):
            total = total + taps[t - m] * curve[m]
        return total

    conc = [convolve(decay, t) for t in range(n_frames)]
    slope = [convolve(drift, t) for t in range(n_frames)]
    power = base_r * base_r + base_i * base_i
    h_aa = power * sum(c * c for c in conc)
    h_ab = power * kt * sum(c * s for c, s in zip(conc, slope))
    h_bb = power * kt * kt * sum(s * s for s in slope)
    d_aa = (1.0 + DAMPING) * h_aa + 1.0
    d_bb = (1.0 + DAMPING) * h_bb + 1.0
    determinant = d_aa * d_bb - h_ab * h_ab

    img_wait()
    g_a = jnp.zeros_like(kt)
    g_b = jnp.zeros_like(kt)
    for t in range(n_frames):
        image = img_recv[t].astype(F32)
        scale = 1.0 + kt * conc[t]
        project = base_r * (image[:height] - base_r * scale) + base_i * (
            image[height:] - base_i * scale
        )
        g_a = g_a + conc[t] * project
        g_b = g_b + slope[t] * project
    g_b = kt * g_b
    step_kt = (d_bb * g_a - h_ab * g_b) / determinant
    step_kp = (d_aa * g_b - h_ab * g_a) / determinant
    kt_next = kt + step_kt
    kp_next = kp + step_kp
    decay = [jnp.exp(-(t * STEP_MINUTES) * kp_next) for t in range(n_frames)]
    for t in range(n_frames):
        image = img_recv[t].astype(F32)
        scale = 1.0 + kt_next * convolve(decay, t)
        res_send[t] = jnp.concatenate(
            [image[:height] - base_r * scale, image[height:] - base_i * scale, step_kt, step_kp], 0
        ).astype(BF16)
    res_start()

    res_wait()
    for e in range(n_frames):
        block = res_recv[e].astype(F32)
        at = 0
        for p in range(4):
            for row, lanes in chunks.pieces(e):
                full[p * rows + row : p * rows + row + chunks.rows, lanes] = block[
                    at : at + chunks.rows
                ]
                at += chunks.rows
    for p in range(2):
        res_out[0, p] = full[p * rows : (p + 1) * rows, :].astype(BF16)
    picked = jnp.dot(
        full[2 * rows :, :].astype(BF16), one_lo[...], preferred_element_type=F32
    )
    in_row = lax.broadcasted_iota(jnp.int32, (rows, voxels), 0) == hi
    kt_out[...] = ktrans[...] + jnp.sum(
        jnp.where(in_row, picked[:rows], 0.0), 0, keepdims=True
    )
    kp_out[...] = kep[...] + jnp.sum(
        jnp.where(in_row, picked[rows:], 0.0), 0, keepdims=True
    )
    for k in range(1, n_coils):
        part_copy(k).wait_send()
    par_drain()
    img_drain()
    res_drain()


def hand_over(*refs):
    count = (len(refs) - 1) // 2
    sems = refs[-1]
    copies = [
        pltpu.make_async_copy(refs[i], refs[count + i], sems.at[i]) for i in range(count)
    ]
    for copy in copies:
        copy.start()
    for copy in copies:
        copy.wait()


def shards(
    kspace,
    sensitivity,
    spoke_count,
    spoke_index,
    band_offset,
    owner_map,
    aif,
    ktrans,
    kep,
    baseline,
):
    n_frames = lax.axis_size("frames")
    n_coils = lax.axis_size("coils")
    _, coils, _, spokes, width = kspace.shape
    voxels = ktrans.shape[1]
    rows = owner_map.shape[1] // width
    height = voxels // LANES
    vmem = pl.BlockSpec(memory_space=pltpu.VMEM)
    hbm = pl.BlockSpec(memory_space=pltpu.HBM)
    operands = (
        kspace,
        sensitivity,
        spoke_count,
        spoke_index,
        band_offset,
        owner_map,
        aif,
        ktrans,
        kep,
        baseline.reshape(2, 1, voxels),
        dft_table(width),
    )
    landing = [
        (pltpu.SMEM if x.ndim == 1 else pltpu.VMEM)(x.shape, x.dtype) for x in operands
    ]
    landing[5] = pltpu.VMEM((n_coils, voxels), jnp.int32)
    pair = pltpu.SemaphoreType.DMA((2, n_frames))
    results = pl.pallas_call(
        functools.partial(kernel, n_frames, n_coils),
        out_shape=[
            jax.ShapeDtypeStruct((1, voxels), F32),
            jax.ShapeDtypeStruct((1, voxels), F32),
            jax.ShapeDtypeStruct((1, 2, rows, width), BF16),
        ],
        in_specs=[hbm] * len(operands),
        out_specs=[vmem, vmem, vmem],
        scratch_shapes=landing
        + [
            pltpu.SemaphoreType.DMA((len(operands),)),
            pltpu.VMEM((width, voxels), BF16),
            pltpu.VMEM((4 * rows, voxels), BF16),
            pltpu.VMEM((width, 2 * spokes), BF16),
            pltpu.VMEM((2 * spokes, coils * 2 * width), BF16),
            pltpu.VMEM((n_coils - 1, 2, rows, width), F32),
            pltpu.VMEM((n_coils - 1, 2, rows, width), F32),
            pltpu.VMEM((n_frames, 4 * height, LANES), BF16),
            pltpu.VMEM((n_frames, 4 * height, LANES), BF16),
            pltpu.VMEM((n_frames, 2 * height, LANES), BF16),
            pltpu.VMEM((n_frames, 2 * height, LANES), BF16),
            pltpu.VMEM((n_frames, 4 * height, LANES), BF16),
            pltpu.VMEM((n_frames, 4 * height, LANES), BF16),
            pltpu.VMEM((4 * rows, width), F32),
            pltpu.SemaphoreType.DMA((2, n_coils)),
            pair,
            pair,
            pair,
        ],
        compiler_params=pltpu.CompilerParams(
            collective_id=0, has_side_effects=True, vmem_limit_bytes=56 * 1024 * 1024
        ),
    )(*operands)
    return pl.pallas_call(
        hand_over,
        out_shape=[jax.ShapeDtypeStruct(x.shape, x.dtype) for x in results],
        in_specs=[hbm] * len(results),
        out_specs=[hbm] * len(results),
        scratch_shapes=[pltpu.SemaphoreType.DMA((len(results),))],
        compiler_params=pltpu.CompilerParams(vmem_limit_bytes=56 * 1024 * 1024),
    )(*results)


def solution(mesh):
    in_specs = (
        P("frames", "coils", None, None, None),
        P("coils", None, None, None),
        P("frames"),
        P("frames", None),
        P("frames", None),
        P(),
        P(),
        P("coils", "frames"),
        P("coils", "frames"),
        P(None, "coils", "frames"),
    )
    out_specs = (P("coils", "frames"), P("coils", "frames"), P("frames", None, "coils", None))
    return jax.shard_map(shards, mesh=mesh, in_specs=in_specs, out_specs=out_specs, check_vma=False)
```

```python
import functools
import math

import jax
import jax.numpy as jnp
import numpy as np
from jax import lax
from jax.experimental import pallas as pl
from jax.experimental.pallas import tpu as pltpu
from jax.sharding import PartitionSpec as P

STEP_MINUTES = 0.05
DAMPING = 0.1
LANES = 128
MESH = pl.DeviceIdType.MESH
F32 = jnp.float32
BF16 = jnp.bfloat16
NT = (((1,), (1,)), ((), ()))


def dft_table(length):
    index = np.arange(length, dtype=np.int64)
    phase = (index[:, None] * index[None, :] % length) * (2.0 * math.pi / length)
    table = np.concatenate([np.cos(phase), np.sin(phase)], 1) / math.sqrt(length)
    return jnp.asarray(table.astype(np.float32)).astype(BF16)


class Chunks:
    def __init__(self, width, voxels):
        self.columns = min(width, voxels)
        self.rows = voxels // self.columns
        self.parts = width // self.columns
        self.height = voxels // LANES

    def pieces(self, number):
        row = number // self.parts * self.rows
        column = number % self.parts * self.columns
        for lane in range(0, self.columns, LANES):
            yield row, slice(column + lane, column + lane + LANES)

    def take(self, plane, number):
        return [plane[row : row + self.rows, lanes] for row, lanes in self.pieces(number)]


def kernel(
    n_frames,
    n_coils,
    kspace_in,
    sens_in,
    count_in,
    spoke_index_in,
    offset_in,
    owner_in,
    aif_in,
    ktrans_in,
    kep_in,
    baseline_in,
    table_in,
    kt_out,
    kp_out,
    res_out,
    kspace,
    sens,
    count,
    spoke_index,
    offset,
    owner,
    aif,
    ktrans,
    kep,
    baseline,
    table,
    input_sems,
    raw_rows,
    raw_send,
    raw_recv,
    one_lo,
    spread,
    left,
    right,
    part_send,
    part_recv,
    par_send,
    par_recv,
    img_send,
    img_recv,
    step_send,
    step_recv,
    res_send,
    res_recv,
    steps,
    pick_rows,
    pick_send,
    pick_recv,
    full,
    part_sems,
    raw_sems,
    par_sems,
    img_sems,
    step_sems,
    res_sems,
    pick_sems,
):
    _, coils, _, spokes, width = kspace.shape
    rows = owner_in.shape[1] // width
    voxels = ktrans.shape[1]
    chunks = Chunks(width, voxels)
    height = chunks.height
    f = lax.axis_index("frames")
    j = lax.axis_index("coils")
    n_lines, n_plane = raw_recv.shape[0], par_recv.shape[0]
    plane_rows = rows // n_lines
    z, q = f // n_plane, lax.rem(f, n_plane)

    def slots(number):
        start = (number * n_plane + q) * voxels
        return pl.ds(pl.multiple_of(start, LANES), voxels)

    loads = {}
    for name, source, target in (
        ("ktrans", ktrans_in, ktrans),
        ("kep", kep_in, kep),
        ("baseline", baseline_in, baseline),
        ("table", table_in, table),
        ("index", spoke_index_in, spoke_index),
        ("offset", offset_in, offset),
        ("count", count_in, count),
        ("kspace", kspace_in, kspace),
        ("sens", sens_in, sens),
        ("aif", aif_in, aif),
        *[
            (b, owner_in.at[:, slots(b)], owner.at[:, b * voxels : (b + 1) * voxels])
            for b in range(n_lines)
        ],
    ):
        loads[name] = pltpu.make_async_copy(source, target, input_sems.at[len(loads)])
        loads[name].start()

    def loaded(*names):
        for name in names:
            loads[name].wait()

    def peer(k):
        return lax.rem(f + k, n_frames)

    def coil_peer(k):
        return lax.rem(j + k, n_coils)

    barrier = pltpu.get_barrier_semaphore()

    def greet(k, _):
        pl.semaphore_signal(
            barrier, inc=1, device_id={"frames": peer(k), "coils": j}, device_id_type=MESH
        )
        return 0

    lax.fori_loop(1, n_frames, greet, 0)
    for k in range(1, n_coils):
        pl.semaphore_signal(
            barrier, inc=1, device_id={"frames": f, "coils": coil_peer(k)}, device_id_type=MESH
        )

    def exchange(send, recv, sems, size, me, device, split):
        def block(number):
            return send.at[number] if split else send

        def copy(k, to, slot):
            return pltpu.make_async_remote_copy(
                src_ref=block(to),
                dst_ref=recv.at[slot],
                send_sem=sems.at[0, k],
                recv_sem=sems.at[1, k],
                device_id={"frames": device(to), "coils": j},
                device_id_type=MESH,
            )

        def start():
            def body(k, _):
                copy(k, lax.rem(me + k, size), me).start()
                return 0

            lax.fori_loop(1, size, body, 0)
            recv[me] = send[me] if split else send[...]

        def wait():
            def body(k, _):
                source = lax.rem(me + size - k, size)
                copy(k, source, source).wait_recv()
                return 0

            lax.fori_loop(1, size, body, 0)

        def drain():
            def body(k, _):
                copy(k, lax.rem(me + k, size), me).wait_send()
                return 0

            lax.fori_loop(1, size, body, 0)

        return start, wait, drain

    line = (n_lines, z, lambda number: number * n_plane + q)
    plane = (n_plane, q, lambda number: z * n_plane + number)
    everyone = (n_frames, f, lambda number: number)
    raw_start, raw_wait, raw_drain = exchange(raw_send, raw_recv, raw_sems, *line, False)
    par_start, par_wait, par_drain = exchange(par_send, par_recv, par_sems, *plane, True)
    img_start, img_wait, img_drain = exchange(img_send, img_recv, img_sems, *everyone, True)
    res_start, res_wait, res_drain = exchange(res_send, res_recv, res_sems, *everyone, True)
    step_start, step_wait, step_drain = exchange(step_send, step_recv, step_sems, *plane, False)
    pick_start, pick_wait, pick_drain = exchange(pick_send, pick_recv, pick_sems, *line, True)

    loaded("ktrans", "kep", "baseline")
    folds, fold = raw_rows.shape[0] // 4, raw_rows.shape[1]
    for p, value in enumerate((ktrans[...], kep[...], baseline[0], baseline[1])):
        for i in range(folds):
            raw_rows[p * folds + i : p * folds + i + 1, :] = value[:, i * fold : (i + 1) * fold]
    raw_send[...] = raw_rows[...].astype(BF16)
    pl.semaphore_wait(barrier, n_frames + n_coils - 2)
    raw_start()

    loaded("index", "offset", "count", "table")
    number = spoke_index[...]
    turn = ((number * 40503) & 65535).astype(F32) * (2.0 * math.pi / 65536.0)
    live = jnp.where(
        lax.broadcasted_iota(jnp.int32, (1, spokes), 1) < count[0], 1.0, 0.0
    ).astype(F32)
    diagonal = lax.broadcasted_iota(jnp.int32, (spokes, spokes), 0) == (
        lax.broadcasted_iota(jnp.int32, (spokes, spokes), 1)
    )

    def column(row):
        return jnp.sum(jnp.where(diagonal, row, 0.0), 1, keepdims=True)

    w_cos = column(live * jnp.cos(turn))
    w_sin = column(live * jnp.sin(turn))
    first = column(offset[...].astype(F32)).astype(jnp.int32)
    tap = lax.broadcasted_iota(jnp.int32, (spokes, width), 1) - first
    band = jnp.where(
        (tap == 0) | (tap == 3), 0.25, jnp.where((tap == 1) | (tap == 2), 0.75, 0.0)
    )
    m_cos = band * w_cos
    m_sin = band * w_sin
    m_a = jnp.concatenate([m_cos, m_sin], 0).astype(BF16)
    m_b = jnp.concatenate([-m_sin, m_cos], 0).astype(BF16)
    left[...] = (
        lax.dot_general(table[:, :width], m_a, NT, preferred_element_type=F32)
        + lax.dot_general(table[:, width:], m_b, NT, preferred_element_type=F32)
    ).astype(BF16)

    loaded("kspace")
    lines = jnp.dot(
        kspace[0].reshape(coils * 2 * spokes, width), table[...], preferred_element_type=F32
    )
    for c in range(coils):
        real = lines[2 * c * spokes : (2 * c + 1) * spokes]
        imag = lines[(2 * c + 1) * spokes : (2 * c + 2) * spokes]
        h_r = (real[:, :width] - imag[:, width:]).astype(BF16)
        h_i = (real[:, width:] + imag[:, :width]).astype(BF16)
        at = 2 * c * width
        right[:spokes, at : at + width] = h_r
        right[:spokes, at + width : at + 2 * width] = h_i
        right[spokes:, at : at + width] = -h_i
        right[spokes:, at + width : at + 2 * width] = h_r

    def partial(which):
        top = pl.multiple_of(which * rows, rows)
        coil_image = jnp.dot(
            left[pl.ds(top, rows), :], right[...], preferred_element_type=F32
        )
        image_r = jnp.zeros((rows, width), F32)
        image_i = jnp.zeros((rows, width), F32)
        for c in range(coils):
            s_r = sens[c, 0, pl.ds(top, rows), :].astype(F32)
            s_i = sens[c, 1, pl.ds(top, rows), :].astype(F32)
            c_r = coil_image[:, 2 * c * width : (2 * c + 1) * width]
            c_i = coil_image[:, (2 * c + 1) * width : (2 * c + 2) * width]
            image_r = image_r + s_r * c_r + s_i * c_i
            image_i = image_i + s_r * c_i - s_i * c_r
        return image_r, image_i

    loaded("sens")

    def part_copy(k):
        return pltpu.make_async_remote_copy(
            src_ref=part_send.at[k - 1],
            dst_ref=part_recv.at[k - 1],
            send_sem=part_sems.at[0, k],
            recv_sem=part_sems.at[1, k],
            device_id={"frames": f, "coils": coil_peer(k)},
            device_id_type=MESH,
        )

    for k in range(1, n_coils):
        image_r, image_i = partial(coil_peer(k))
        part_send[k - 1, 0] = image_r
        part_send[k - 1, 1] = image_i
        part_copy(k).start()

    loaded(*range(n_lines))
    place = owner[0:1, :]
    for c in range(1, n_coils):
        place = jnp.where(j == c, owner[c : c + 1, :], place)
    lo = place & (width - 1)
    hi = lax.shift_right_logical(place, int(math.log2(width))) - z * plane_rows
    for b in range(n_lines):
        cut = slice(b * voxels, (b + 1) * voxels)
        one_lo[:, cut] = jnp.where(
            lax.broadcasted_iota(jnp.int32, (width, voxels), 0) == lo[:, cut], 1.0, 0.0
        ).astype(BF16)
    raw_wait()
    for b in range(n_lines):
        block = raw_recv[b].astype(F32)
        for i in range(folds):
            cut = slice(b * voxels + i * fold, b * voxels + (i + 1) * fold)
            in_row = lax.broadcasted_iota(jnp.int32, (plane_rows, fold), 0) == hi[:, cut]
            spread[:, cut] = jnp.concatenate(
                [
                    jnp.where(in_row, block[p * folds + i : p * folds + i + 1], 0.0)
                    for p in range(4)
                ],
                0,
            ).astype(BF16)
    placed = lax.dot_general(spread[...], one_lo[...], NT, preferred_element_type=F32)
    for e in range(n_plane):
        pieces = []
        for p in range(4):
            pieces += chunks.take(placed[p * plane_rows : (p + 1) * plane_rows], e)
        par_send[e] = jnp.concatenate(pieces, 0).astype(BF16)
    par_start()

    image_r, image_i = partial(j)
    for k in range(1, n_coils):
        part_copy(k).wait_recv()
        image_r = image_r + part_recv[k - 1, 0]
        image_i = image_i + part_recv[k - 1, 1]
    for e in range(n_frames):
        pieces = chunks.take(image_r, e) + chunks.take(image_i, e)
        img_send[e] = jnp.concatenate(pieces, 0).astype(BF16)
    img_start()

    par_wait()
    params = par_recv[0].astype(F32)
    for e in range(1, n_plane):
        params = params + par_recv[e].astype(F32)
    kt, kp, base_r, base_i = [params[p * height : (p + 1) * height] for p in range(4)]
    loaded("aif")
    taps = [aif[t] * STEP_MINUTES for t in range(n_frames)]
    decay = [jnp.exp(-(t * STEP_MINUTES) * kp) for t in range(n_frames)]
    drift = [decay[t] * -(t * STEP_MINUTES) for t in range(n_frames)]

    def convolve(curve, t):
        total = taps[t] * curve[0]
        for m in range(1, t + 1):
            total = total + taps[t - m] * curve[m]
        return total

    conc = [convolve(decay, t) for t in range(n_frames)]
    slope = [convolve(drift, t) for t in range(n_frames)]
    power = base_r * base_r + base_i * base_i
    h_aa = power * sum(c * c for c in conc)
    h_ab = power * kt * sum(c * s for c, s in zip(conc, slope))
    h_bb = power * kt * kt * sum(s * s for s in slope)
    d_aa = (1.0 + DAMPING) * h_aa + 1.0
    d_bb = (1.0 + DAMPING) * h_bb + 1.0
    determinant = d_aa * d_bb - h_ab * h_ab

    img_wait()
    g_a = jnp.zeros_like(kt)
    g_b = jnp.zeros_like(kt)
    for t in range(n_frames):
        image = img_recv[t].astype(F32)
        scale = 1.0 + kt * conc[t]
        project = base_r * (image[:height] - base_r * scale) + base_i * (
            image[height:] - base_i * scale
        )
        g_a = g_a + conc[t] * project
        g_b = g_b + slope[t] * project
    g_b = kt * g_b
    step_kt = (d_bb * g_a - h_ab * g_b) / determinant
    step_kp = (d_aa * g_b - h_ab * g_a) / determinant
    step_send[...] = jnp.concatenate([step_kt, step_kp], 0).astype(BF16)
    step_start()
    kt_next = kt + step_kt
    kp_next = kp + step_kp
    decay = [jnp.exp(-(t * STEP_MINUTES) * kp_next) for t in range(n_frames)]
    for t in range(n_frames):
        image = img_recv[t].astype(F32)
        scale = 1.0 + kt_next * convolve(decay, t)
        res_send[t] = jnp.concatenate(
            [image[:height] - base_r * scale, image[height:] - base_i * scale], 0
        ).astype(BF16)
    res_start()

    def unpack(block, target, stride, number, planes):
        at = 0
        for p in range(planes):
            for row, lanes in chunks.pieces(number):
                top = p * stride + row
                target[top : top + chunks.rows, lanes] = block[at : at + chunks.rows]
                at += chunks.rows

    step_wait()
    for e in range(n_plane):
        unpack(step_recv[e].astype(F32), steps, plane_rows, e, 2)
    pick_folds, pick_fold = pick_rows.shape[0] // 2, pick_rows.shape[1]
    for b in range(n_lines):
        cut = slice(b * voxels, (b + 1) * voxels)
        picked = jnp.dot(
            steps[...].astype(BF16), one_lo[:, cut], preferred_element_type=F32
        )
        in_row = lax.broadcasted_iota(jnp.int32, (plane_rows, voxels), 0) == hi[:, cut]
        for p in range(2):
            chosen = jnp.sum(
                jnp.where(in_row, picked[p * plane_rows : (p + 1) * plane_rows], 0.0),
                0,
                keepdims=True,
            )
            for i in range(pick_folds):
                pick_rows[p * pick_folds + i : p * pick_folds + i + 1, :] = chosen[
                    :, i * pick_fold : (i + 1) * pick_fold
                ]
        pick_send[b] = pick_rows[...].astype(BF16)
    pick_start()

    res_wait()
    for e in range(n_frames):
        unpack(res_recv[e].astype(F32), full, rows, e, 2)
    for p in range(2):
        res_out[0, p] = full[p * rows : (p + 1) * rows, :].astype(BF16)
    pick_wait()
    total = pick_recv[0].astype(F32)
    for b in range(1, n_lines):
        total = total + pick_recv[b].astype(F32)
    for p, (old, new) in enumerate(((ktrans, kt_out), (kep, kp_out))):
        for i in range(pick_folds):
            cut = slice(i * pick_fold, (i + 1) * pick_fold)
            row = p * pick_folds + i
            new[:, cut] = old[:, cut] + total[row : row + 1]
    for k in range(1, n_coils):
        part_copy(k).wait_send()
    raw_drain()
    par_drain()
    img_drain()
    step_drain()
    res_drain()
    pick_drain()


def hand_over(*refs):
    count = len(refs) // 3
    sems = refs[-1]
    into, out = [], []
    for i in range(count):
        held = refs[2 * count + i]
        into.append(pltpu.make_async_copy(refs[i], held, sems.at[0, i]))
        out.append(pltpu.make_async_copy(held, refs[count + i], sems.at[1, i]))
    for copy in into:
        copy.start()
    for i in range(count):
        into[i].wait()
        out[i].start()
    for copy in out:
        copy.wait()


def shards(
    kspace,
    sensitivity,
    spoke_count,
    spoke_index,
    band_offset,
    owner_map,
    aif,
    ktrans,
    kep,
    baseline,
):
    n_frames = lax.axis_size("frames")
    n_coils = lax.axis_size("coils")
    _, coils, _, spokes, width = kspace.shape
    voxels = ktrans.shape[1]
    rows = owner_map.shape[1] // width
    height = voxels // LANES
    n_plane = 1
    while n_plane * n_plane < n_frames:
        n_plane *= 2
    n_lines = n_frames // n_plane
    plane_rows = rows // n_lines
    folds = 4 if voxels % (4 * LANES) == 0 else 1
    pick_folds = 8 if voxels % (8 * LANES) == 0 else 1
    vmem = pl.BlockSpec(memory_space=pltpu.VMEM)
    hbm = pl.BlockSpec(memory_space=pltpu.HBM)
    operands = (
        kspace,
        sensitivity,
        spoke_count,
        spoke_index,
        band_offset,
        owner_map,
        aif,
        ktrans,
        kep,
        baseline.reshape(2, 1, voxels),
        dft_table(width),
    )
    landing = [
        (pltpu.SMEM if x.ndim == 1 else pltpu.VMEM)(x.shape, x.dtype) for x in operands
    ]
    landing[5] = pltpu.VMEM((n_coils, n_lines * voxels), jnp.int32)
    results = pl.pallas_call(
        functools.partial(kernel, n_frames, n_coils),
        out_shape=[
            jax.ShapeDtypeStruct((1, voxels), F32),
            jax.ShapeDtypeStruct((1, voxels), F32),
            jax.ShapeDtypeStruct((1, 2, rows, width), BF16),
        ],
        in_specs=[hbm] * len(operands),
        out_specs=[vmem, vmem, vmem],
        scratch_shapes=landing
        + [
            pltpu.SemaphoreType.DMA((len(operands) - 1 + n_lines,)),
            pltpu.VMEM((4 * folds, voxels // folds), F32),
            pltpu.VMEM((4 * folds, voxels // folds), BF16),
            pltpu.VMEM((n_lines, 4 * folds, voxels // folds), BF16),
            pltpu.VMEM((width, n_lines * voxels), BF16),
            pltpu.VMEM((4 * plane_rows, n_lines * voxels), BF16),
            pltpu.VMEM((width, 2 * spokes), BF16),
            pltpu.VMEM((2 * spokes, coils * 2 * width), BF16),
            pltpu.VMEM((n_coils - 1, 2, rows, width), F32),
            pltpu.VMEM((n_coils - 1, 2, rows, width), F32),
            pltpu.VMEM((n_plane, 4 * height, LANES), BF16),
            pltpu.VMEM((n_plane, 4 * height, LANES), BF16),
            pltpu.VMEM((n_frames, 2 * height, LANES), BF16),
            pltpu.VMEM((n_frames, 2 * height, LANES), BF16),
            pltpu.VMEM((2 * height, LANES), BF16),
            pltpu.VMEM((n_plane, 2 * height, LANES), BF16),
            pltpu.VMEM((n_frames, 2 * height, LANES), BF16),
            pltpu.VMEM((n_frames, 2 * height, LANES), BF16),
            pltpu.VMEM((2 * plane_rows, width), F32),
            pltpu.VMEM((2 * pick_folds, voxels // pick_folds), F32),
            pltpu.VMEM((n_lines, 2 * pick_folds, voxels // pick_folds), BF16),
            pltpu.VMEM((n_lines, 2 * pick_folds, voxels // pick_folds), BF16),
            pltpu.VMEM((2 * rows, width), F32),
            pltpu.SemaphoreType.DMA((2, n_coils)),
            pltpu.SemaphoreType.DMA((2, n_lines)),
            pltpu.SemaphoreType.DMA((2, n_plane)),
            pltpu.SemaphoreType.DMA((2, n_frames)),
            pltpu.SemaphoreType.DMA((2, n_plane)),
            pltpu.SemaphoreType.DMA((2, n_frames)),
            pltpu.SemaphoreType.DMA((2, n_lines)),
        ],
        compiler_params=pltpu.CompilerParams(
            collective_id=0, has_side_effects=True, vmem_limit_bytes=56 * 1024 * 1024
        ),
    )(*operands)
    return pl.pallas_call(
        hand_over,
        out_shape=[jax.ShapeDtypeStruct(x.shape, x.dtype) for x in results],
        in_specs=[hbm] * len(results),
        out_specs=[hbm] * len(results),
        scratch_shapes=[pltpu.VMEM(x.shape, x.dtype) for x in results]
        + [pltpu.SemaphoreType.DMA((2, len(results)))],
        compiler_params=pltpu.CompilerParams(vmem_limit_bytes=56 * 1024 * 1024),
    )(*results)


def solution(mesh):
    in_specs = (
        P("frames", "coils", None, None, None),
        P("coils", None, None, None),
        P("frames"),
        P("frames", None),
        P("frames", None),
        P(),
        P(),
        P("coils", "frames"),
        P("coils", "frames"),
        P(None, "coils", "frames"),
    )
    out_specs = (P("coils", "frames"), P("coils", "frames"), P("frames", None, "coils", None))
    return jax.shard_map(shards, mesh=mesh, in_specs=in_specs, out_specs=out_specs, check_vma=False)
```

```python
import functools
import math

import jax
import jax.numpy as jnp
import numpy as np
from jax import lax
from jax.experimental import pallas as pl
from jax.experimental.pallas import tpu as pltpu
from jax.sharding import PartitionSpec as P

STEP_MINUTES = 0.05
DAMPING = 0.1
LANES = 128
MESH = pl.DeviceIdType.MESH
F32 = jnp.float32
BF16 = jnp.bfloat16
NT = (((1,), (1,)), ((), ()))


def dft_table(length):
    index = np.arange(length, dtype=np.int64)
    phase = (index[:, None] * index[None, :] % length) * (2.0 * math.pi / length)
    table = np.concatenate([np.cos(phase), np.sin(phase)], 1) / math.sqrt(length)
    return jnp.asarray(table.astype(np.float32)).astype(BF16)


class Chunks:
    def __init__(self, width, voxels):
        self.columns = min(width, voxels)
        self.rows = voxels // self.columns
        self.parts = width // self.columns
        self.height = voxels // LANES

    def pieces(self, number):
        row = number // self.parts * self.rows
        column = number % self.parts * self.columns
        for lane in range(0, self.columns, LANES):
            yield row, slice(column + lane, column + lane + LANES)

    def take(self, plane, number):
        return [plane[row : row + self.rows, lanes] for row, lanes in self.pieces(number)]


def kernel(
    n_frames,
    n_coils,
    kspace_in,
    sens_in,
    count_in,
    spoke_index_in,
    offset_in,
    owner_in,
    aif_in,
    ktrans_in,
    kep_in,
    baseline_in,
    table_in,
    kt_out,
    kp_out,
    res_out,
    kspace,
    sens,
    count,
    spoke_index,
    offset,
    owner,
    aif,
    ktrans,
    kep,
    baseline,
    table,
    input_sems,
    raw_rows,
    raw_send,
    raw_recv,
    one_lo,
    spread,
    left,
    right,
    part_send,
    part_recv,
    par_send,
    par_recv,
    img_send,
    img_recv,
    step_send,
    step_recv,
    res_send,
    res_recv,
    own_hi,
    full,
    part_sems,
    raw_sems,
    par_sems,
    img_sems,
    step_sems,
    res_sems,
):
    _, coils, _, spokes, width = kspace.shape
    rows = owner_in.shape[1] // width
    voxels = ktrans.shape[1]
    chunks = Chunks(width, voxels)
    height = chunks.height
    f = lax.axis_index("frames")
    j = lax.axis_index("coils")
    n_lines, n_plane = raw_recv.shape[0], par_recv.shape[0]
    plane_rows = rows // n_lines
    z, q = f // n_plane, lax.rem(f, n_plane)

    def slots(number):
        start = (number * n_plane + q) * voxels
        return pl.ds(pl.multiple_of(start, LANES), voxels)

    loads = {}
    for name, source, target in (
        ("ktrans", ktrans_in, ktrans),
        ("kep", kep_in, kep),
        ("baseline", baseline_in, baseline),
        ("table", table_in, table),
        ("index", spoke_index_in, spoke_index),
        ("offset", offset_in, offset),
        ("count", count_in, count),
        ("kspace", kspace_in, kspace),
        ("sens", sens_in, sens),
        ("aif", aif_in, aif),
        *[
            (b, owner_in.at[:, slots(b)], owner.at[:, b * voxels : (b + 1) * voxels])
            for b in range(n_lines)
        ],
    ):
        loads[name] = pltpu.make_async_copy(source, target, input_sems.at[len(loads)])
        loads[name].start()

    def loaded(*names):
        for name in names:
            loads[name].wait()

    def peer(k):
        return lax.rem(f + k, n_frames)

    def coil_peer(k):
        return lax.rem(j + k, n_coils)

    barrier = pltpu.get_barrier_semaphore()

    def greet(k, _):
        pl.semaphore_signal(
            barrier, inc=1, device_id={"frames": peer(k), "coils": j}, device_id_type=MESH
        )
        return 0

    lax.fori_loop(1, n_frames, greet, 0)
    for k in range(1, n_coils):
        pl.semaphore_signal(
            barrier, inc=1, device_id={"frames": f, "coils": coil_peer(k)}, device_id_type=MESH
        )

    def exchange(send, recv, sems, size, me, device, split):
        def block(number):
            return send.at[number] if split else send

        def copy(k, to, slot):
            return pltpu.make_async_remote_copy(
                src_ref=block(to),
                dst_ref=recv.at[slot],
                send_sem=sems.at[0, k],
                recv_sem=sems.at[1, k],
                device_id={"frames": device(to), "coils": j},
                device_id_type=MESH,
            )

        def start():
            def body(k, _):
                copy(k, lax.rem(me + k, size), me).start()
                return 0

            lax.fori_loop(1, size, body, 0)
            recv[me] = send[me] if split else send[...]

        def wait():
            def body(k, _):
                source = lax.rem(me + size - k, size)
                copy(k, source, source).wait_recv()
                return 0

            lax.fori_loop(1, size, body, 0)

        def drain():
            def body(k, _):
                copy(k, lax.rem(me + k, size), me).wait_send()
                return 0

            lax.fori_loop(1, size, body, 0)

        return start, wait, drain

    line = (n_lines, z, lambda number: number * n_plane + q)
    plane = (n_plane, q, lambda number: z * n_plane + number)
    everyone = (n_frames, f, lambda number: number)
    raw_start, raw_wait, raw_drain = exchange(raw_send, raw_recv, raw_sems, *line, False)
    par_start, par_wait, par_drain = exchange(par_send, par_recv, par_sems, *plane, True)
    img_start, img_wait, img_drain = exchange(img_send, img_recv, img_sems, *everyone, True)
    res_start, res_wait, res_drain = exchange(res_send, res_recv, res_sems, *everyone, True)
    step_start, step_wait, step_drain = exchange(step_send, step_recv, step_sems, *everyone, False)

    loaded("ktrans", "kep", "baseline")
    folds, fold = raw_rows.shape[0] // 4, raw_rows.shape[1]
    for p, value in enumerate((ktrans[...], kep[...], baseline[0], baseline[1])):
        for i in range(folds):
            raw_rows[p * folds + i : p * folds + i + 1, :] = value[:, i * fold : (i + 1) * fold]
    raw_send[...] = raw_rows[...].astype(BF16)
    pl.semaphore_wait(barrier, n_frames + n_coils - 2)
    raw_start()

    loaded("index", "offset", "count", "table")
    number = spoke_index[...]
    turn = ((number * 40503) & 65535).astype(F32) * (2.0 * math.pi / 65536.0)
    live = jnp.where(
        lax.broadcasted_iota(jnp.int32, (1, spokes), 1) < count[0], 1.0, 0.0
    ).astype(F32)
    diagonal = lax.broadcasted_iota(jnp.int32, (spokes, spokes), 0) == (
        lax.broadcasted_iota(jnp.int32, (spokes, spokes), 1)
    )

    def column(row):
        return jnp.sum(jnp.where(diagonal, row, 0.0), 1, keepdims=True)

    w_cos = column(live * jnp.cos(turn))
    w_sin = column(live * jnp.sin(turn))
    first = column(offset[...].astype(F32)).astype(jnp.int32)
    tap = lax.broadcasted_iota(jnp.int32, (spokes, width), 1) - first
    band = jnp.where(
        (tap == 0) | (tap == 3), 0.25, jnp.where((tap == 1) | (tap == 2), 0.75, 0.0)
    )
    m_cos = band * w_cos
    m_sin = band * w_sin
    m_a = jnp.concatenate([m_cos, m_sin], 0).astype(BF16)
    m_b = jnp.concatenate([-m_sin, m_cos], 0).astype(BF16)
    left[...] = (
        lax.dot_general(table[:, :width], m_a, NT, preferred_element_type=F32)
        + lax.dot_general(table[:, width:], m_b, NT, preferred_element_type=F32)
    ).astype(BF16)

    loaded("kspace")
    lines = jnp.dot(
        kspace[0].reshape(coils * 2 * spokes, width), table[...], preferred_element_type=F32
    )
    for c in range(coils):
        real = lines[2 * c * spokes : (2 * c + 1) * spokes]
        imag = lines[(2 * c + 1) * spokes : (2 * c + 2) * spokes]
        h_r = (real[:, :width] - imag[:, width:]).astype(BF16)
        h_i = (real[:, width:] + imag[:, :width]).astype(BF16)
        at = 2 * c * width
        right[:spokes, at : at + width] = h_r
        right[:spokes, at + width : at + 2 * width] = h_i
        right[spokes:, at : at + width] = -h_i
        right[spokes:, at + width : at + 2 * width] = h_r

    def partial(which):
        top = pl.multiple_of(which * rows, rows)
        coil_image = jnp.dot(
            left[pl.ds(top, rows), :], right[...], preferred_element_type=F32
        )
        image_r = jnp.zeros((rows, width), F32)
        image_i = jnp.zeros((rows, width), F32)
        for c in range(coils):
            s_r = sens[c, 0, pl.ds(top, rows), :].astype(F32)
            s_i = sens[c, 1, pl.ds(top, rows), :].astype(F32)
            c_r = coil_image[:, 2 * c * width : (2 * c + 1) * width]
            c_i = coil_image[:, (2 * c + 1) * width : (2 * c + 2) * width]
            image_r = image_r + s_r * c_r + s_i * c_i
            image_i = image_i + s_r * c_i - s_i * c_r
        return image_r, image_i

    loaded("sens")

    def part_copy(k):
        return pltpu.make_async_remote_copy(
            src_ref=part_send.at[k - 1],
            dst_ref=part_recv.at[k - 1],
            send_sem=part_sems.at[0, k],
            recv_sem=part_sems.at[1, k],
            device_id={"frames": f, "coils": coil_peer(k)},
            device_id_type=MESH,
        )

    for k in range(1, n_coils):
        image_r, image_i = partial(coil_peer(k))
        part_send[k - 1, 0] = image_r
        part_send[k - 1, 1] = image_i
        part_copy(k).start()

    loaded(*range(n_lines))
    place = owner[0:1, :]
    for c in range(1, n_coils):
        place = jnp.where(j == c, owner[c : c + 1, :], place)
    lo = place & (width - 1)
    hi = lax.shift_right_logical(place, int(math.log2(width)))
    own_hi[...] = hi[:, :voxels]
    for b in range(1, n_lines):
        own_hi[...] = jnp.where(z == b, hi[:, b * voxels : (b + 1) * voxels], own_hi[...])
    hi = hi - z * plane_rows
    for b in range(n_lines):
        cut = slice(b * voxels, (b + 1) * voxels)
        one_lo[:, cut] = jnp.where(
            lax.broadcasted_iota(jnp.int32, (width, voxels), 0) == lo[:, cut], 1.0, 0.0
        ).astype(BF16)
    raw_wait()
    for b in range(n_lines):
        block = raw_recv[b].astype(F32)
        for i in range(folds):
            cut = slice(b * voxels + i * fold, b * voxels + (i + 1) * fold)
            in_row = lax.broadcasted_iota(jnp.int32, (plane_rows, fold), 0) == hi[:, cut]
            spread[:, cut] = jnp.concatenate(
                [
                    jnp.where(in_row, block[p * folds + i : p * folds + i + 1], 0.0)
                    for p in range(4)
                ],
                0,
            ).astype(BF16)
    placed = lax.dot_general(spread[...], one_lo[...], NT, preferred_element_type=F32)
    for e in range(n_plane):
        pieces = []
        for p in range(4):
            pieces += chunks.take(placed[p * plane_rows : (p + 1) * plane_rows], e)
        par_send[e] = jnp.concatenate(pieces, 0).astype(BF16)
    par_start()

    image_r, image_i = partial(j)
    for k in range(1, n_coils):
        part_copy(k).wait_recv()
        image_r = image_r + part_recv[k - 1, 0]
        image_i = image_i + part_recv[k - 1, 1]
    for e in range(n_frames):
        pieces = chunks.take(image_r, e) + chunks.take(image_i, e)
        img_send[e] = jnp.concatenate(pieces, 0).astype(BF16)
    img_start()

    par_wait()
    params = par_recv[0].astype(F32)
    for e in range(1, n_plane):
        params = params + par_recv[e].astype(F32)
    kt, kp, base_r, base_i = [params[p * height : (p + 1) * height] for p in range(4)]
    loaded("aif")
    taps = [aif[t] * STEP_MINUTES for t in range(n_frames)]
    decay = [jnp.exp(-(t * STEP_MINUTES) * kp) for t in range(n_frames)]
    drift = [decay[t] * -(t * STEP_MINUTES) for t in range(n_frames)]

    def convolve(curve, t):
        total = taps[t] * curve[0]
        for m in range(1, t + 1):
            total = total + taps[t - m] * curve[m]
        return total

    conc = [convolve(decay, t) for t in range(n_frames)]
    slope = [convolve(drift, t) for t in range(n_frames)]
    power = base_r * base_r + base_i * base_i
    h_aa = power * sum(c * c for c in conc)
    h_ab = power * kt * sum(c * s for c, s in zip(conc, slope))
    h_bb = power * kt * kt * sum(s * s for s in slope)
    d_aa = (1.0 + DAMPING) * h_aa + 1.0
    d_bb = (1.0 + DAMPING) * h_bb + 1.0
    determinant = d_aa * d_bb - h_ab * h_ab

    img_wait()
    g_a = jnp.zeros_like(kt)
    g_b = jnp.zeros_like(kt)
    for t in range(n_frames):
        image = img_recv[t].astype(F32)
        scale = 1.0 + kt * conc[t]
        project = base_r * (image[:height] - base_r * scale) + base_i * (
            image[height:] - base_i * scale
        )
        g_a = g_a + conc[t] * project
        g_b = g_b + slope[t] * project
    g_b = kt * g_b
    step_kt = (d_bb * g_a - h_ab * g_b) / determinant
    step_kp = (d_aa * g_b - h_ab * g_a) / determinant
    step_send[...] = jnp.concatenate([step_kt, step_kp], 0).astype(BF16)
    step_start()
    kt_next = kt + step_kt
    kp_next = kp + step_kp
    decay = [jnp.exp(-(t * STEP_MINUTES) * kp_next) for t in range(n_frames)]
    for t in range(n_frames):
        image = img_recv[t].astype(F32)
        scale = 1.0 + kt_next * convolve(decay, t)
        res_send[t] = jnp.concatenate(
            [image[:height] - base_r * scale, image[height:] - base_i * scale], 0
        ).astype(BF16)
    res_start()

    def unpack(block, target, number):
        at = 0
        for p in range(2):
            for row, lanes in chunks.pieces(number):
                top = p * rows + row
                target[top : top + chunks.rows, lanes] = block[at : at + chunks.rows]
                at += chunks.rows

    step_wait()
    for e in range(n_frames):
        unpack(step_recv[e].astype(F32), full, e)
    own_cut = pl.ds(pl.multiple_of(z * voxels, LANES), voxels)
    picked = jnp.dot(
        full[...].astype(BF16), one_lo[:, own_cut], preferred_element_type=F32
    )
    in_row = lax.broadcasted_iota(jnp.int32, (rows, voxels), 0) == own_hi[...]
    for p, (old, new) in enumerate(((ktrans, kt_out), (kep, kp_out))):
        new[...] = old[...] + jnp.sum(
            jnp.where(in_row, picked[p * rows : (p + 1) * rows], 0.0), 0, keepdims=True
        )

    res_wait()
    for e in range(n_frames):
        unpack(res_recv[e].astype(F32), full, e)
    for p in range(2):
        res_out[0, p] = full[p * rows : (p + 1) * rows, :].astype(BF16)
    for k in range(1, n_coils):
        part_copy(k).wait_send()
    raw_drain()
    par_drain()
    img_drain()
    step_drain()
    res_drain()


def hand_over(*refs):
    count = len(refs) // 3
    sems = refs[-1]
    into, out = [], []
    for i in range(count):
        held = refs[2 * count + i]
        into.append(pltpu.make_async_copy(refs[i], held, sems.at[0, i]))
        out.append(pltpu.make_async_copy(held, refs[count + i], sems.at[1, i]))
    for copy in into:
        copy.start()
    for i in range(count):
        into[i].wait()
        out[i].start()
    for copy in out:
        copy.wait()


def shards(
    kspace,
    sensitivity,
    spoke_count,
    spoke_index,
    band_offset,
    owner_map,
    aif,
    ktrans,
    kep,
    baseline,
):
    n_frames = lax.axis_size("frames")
    n_coils = lax.axis_size("coils")
    _, coils, _, spokes, width = kspace.shape
    voxels = ktrans.shape[1]
    rows = owner_map.shape[1] // width
    height = voxels // LANES
    n_plane = 1
    while n_plane * n_plane < n_frames:
        n_plane *= 2
    n_lines = n_frames // n_plane
    plane_rows = rows // n_lines
    folds = 4 if voxels % (4 * LANES) == 0 else 1
    vmem = pl.BlockSpec(memory_space=pltpu.VMEM)
    hbm = pl.BlockSpec(memory_space=pltpu.HBM)
    operands = (
        kspace,
        sensitivity,
        spoke_count,
        spoke_index,
        band_offset,
        owner_map,
        aif,
        ktrans,
        kep,
        baseline.reshape(2, 1, voxels),
        dft_table(width),
    )
    landing = [
        (pltpu.SMEM if x.ndim == 1 else pltpu.VMEM)(x.shape, x.dtype) for x in operands
    ]
    landing[5] = pltpu.VMEM((n_coils, n_lines * voxels), jnp.int32)
    results = pl.pallas_call(
        functools.partial(kernel, n_frames, n_coils),
        out_shape=[
            jax.ShapeDtypeStruct((1, voxels), F32),
            jax.ShapeDtypeStruct((1, voxels), F32),
            jax.ShapeDtypeStruct((1, 2, rows, width), BF16),
        ],
        in_specs=[hbm] * len(operands),
        out_specs=[vmem, vmem, vmem],
        scratch_shapes=landing
        + [
            pltpu.SemaphoreType.DMA((len(operands) - 1 + n_lines,)),
            pltpu.VMEM((4 * folds, voxels // folds), F32),
            pltpu.VMEM((4 * folds, voxels // folds), BF16),
            pltpu.VMEM((n_lines, 4 * folds, voxels // folds), BF16),
            pltpu.VMEM((width, n_lines * voxels), BF16),
            pltpu.VMEM((4 * plane_rows, n_lines * voxels), BF16),
            pltpu.VMEM((width, 2 * spokes), BF16),
            pltpu.VMEM((2 * spokes, coils * 2 * width), BF16),
            pltpu.VMEM((n_coils - 1, 2, rows, width), F32),
            pltpu.VMEM((n_coils - 1, 2, rows, width), F32),
            pltpu.VMEM((n_plane, 4 * height, LANES), BF16),
            pltpu.VMEM((n_plane, 4 * height, LANES), BF16),
            pltpu.VMEM((n_frames, 2 * height, LANES), BF16),
            pltpu.VMEM((n_frames, 2 * height, LANES), BF16),
            pltpu.VMEM((2 * height, LANES), BF16),
            pltpu.VMEM((n_frames, 2 * height, LANES), BF16),
            pltpu.VMEM((n_frames, 2 * height, LANES), BF16),
            pltpu.VMEM((n_frames, 2 * height, LANES), BF16),
            pltpu.VMEM((1, voxels), jnp.int32),
            pltpu.VMEM((2 * rows, width), F32),
            pltpu.SemaphoreType.DMA((2, n_coils)),
            pltpu.SemaphoreType.DMA((2, n_lines)),
            pltpu.SemaphoreType.DMA((2, n_plane)),
            pltpu.SemaphoreType.DMA((2, n_frames)),
            pltpu.SemaphoreType.DMA((2, n_frames)),
            pltpu.SemaphoreType.DMA((2, n_frames)),
        ],
        compiler_params=pltpu.CompilerParams(
            collective_id=0, has_side_effects=True, vmem_limit_bytes=56 * 1024 * 1024
        ),
    )(*operands)
    return pl.pallas_call(
        hand_over,
        out_shape=[jax.ShapeDtypeStruct(x.shape, x.dtype) for x in results],
        in_specs=[hbm] * len(results),
        out_specs=[hbm] * len(results),
        scratch_shapes=[pltpu.VMEM(x.shape, x.dtype) for x in results]
        + [pltpu.SemaphoreType.DMA((2, len(results)))],
        compiler_params=pltpu.CompilerParams(vmem_limit_bytes=56 * 1024 * 1024),
    )(*results)


def solution(mesh):
    in_specs = (
        P("frames", "coils", None, None, None),
        P("coils", None, None, None),
        P("frames"),
        P("frames", None),
        P("frames", None),
        P(),
        P(),
        P("coils", "frames"),
        P("coils", "frames"),
        P(None, "coils", "frames"),
    )
    out_specs = (P("coils", "frames"), P("coils", "frames"), P("frames", None, "coils", None))
    return jax.shard_map(shards, mesh=mesh, in_specs=in_specs, out_specs=out_specs, check_vma=False)
```

```python
import functools
import math

import jax
import jax.numpy as jnp
import numpy as np
from jax import lax
from jax.experimental import pallas as pl
from jax.experimental.pallas import tpu as pltpu
from jax.sharding import PartitionSpec as P

STEP_MINUTES = 0.05
DAMPING = 0.1
LANES = 128
MESH = pl.DeviceIdType.MESH
F32 = jnp.float32
BF16 = jnp.bfloat16
NT = (((1,), (1,)), ((), ()))


def dft_table(length):
    index = np.arange(length, dtype=np.int64)
    phase = (index[:, None] * index[None, :] % length) * (2.0 * math.pi / length)
    table = np.concatenate([np.cos(phase), np.sin(phase)], 1) / math.sqrt(length)
    return jnp.asarray(table.astype(np.float32)).astype(BF16)


class Chunks:
    def __init__(self, width, voxels):
        self.columns = min(width, voxels)
        self.rows = voxels // self.columns
        self.parts = width // self.columns
        self.height = voxels // LANES

    def pieces(self, number):
        row = number // self.parts * self.rows
        column = number % self.parts * self.columns
        for lane in range(0, self.columns, LANES):
            yield row, slice(column + lane, column + lane + LANES)

    def take(self, plane, number):
        return [plane[row : row + self.rows, lanes] for row, lanes in self.pieces(number)]


def kernel(
    n_frames,
    n_coils,
    kspace_in,
    sens_in,
    count_in,
    spoke_index_in,
    offset_in,
    owner_in,
    aif_in,
    ktrans_in,
    kep_in,
    baseline_in,
    table_in,
    kt_out,
    kp_out,
    res_out,
    kspace,
    sens,
    count,
    spoke_index,
    offset,
    owner,
    aif,
    ktrans,
    kep,
    baseline,
    table,
    input_sems,
    raw_rows,
    raw_send,
    raw_recv,
    one_lo,
    spread,
    left,
    right,
    part_send,
    part_recv,
    par_send,
    par_recv,
    img_send,
    img_recv,
    step_send,
    step_recv,
    res_send,
    res_recv,
    own_hi,
    full,
    part_sems,
    raw_sems,
    par_sems,
    img_sems,
    step_sems,
    res_sems,
):
    _, coils, _, spokes, width = kspace.shape
    rows = owner_in.shape[1] // width
    voxels = ktrans.shape[1]
    chunks = Chunks(width, voxels)
    height = chunks.height
    f = lax.axis_index("frames")
    j = lax.axis_index("coils")
    n_lines, n_plane = raw_recv.shape[0], par_recv.shape[0]
    plane_rows = rows // n_lines
    z, q = f // n_plane, lax.rem(f, n_plane)

    def slots(number):
        start = (number * n_plane + q) * voxels
        return pl.ds(pl.multiple_of(start, LANES), voxels)

    loads = {}
    for name, source, target in (
        ("ktrans", ktrans_in, ktrans),
        ("kep", kep_in, kep),
        ("baseline", baseline_in, baseline),
        ("table", table_in, table),
        ("index", spoke_index_in, spoke_index),
        ("offset", offset_in, offset),
        ("count", count_in, count),
        ("kspace", kspace_in, kspace),
        ("sens", sens_in, sens),
        ("aif", aif_in, aif),
        *[
            (b, owner_in.at[:, slots(b)], owner.at[:, b * voxels : (b + 1) * voxels])
            for b in range(n_lines)
        ],
    ):
        loads[name] = pltpu.make_async_copy(source, target, input_sems.at[len(loads)])
        loads[name].start()

    def loaded(*names):
        for name in names:
            loads[name].wait()

    def peer(k):
        return lax.rem(f + k, n_frames)

    def coil_peer(k):
        return lax.rem(j + k, n_coils)

    barrier = pltpu.get_barrier_semaphore()

    def greet(k, _):
        pl.semaphore_signal(
            barrier, inc=1, device_id={"frames": peer(k), "coils": j}, device_id_type=MESH
        )
        return 0

    lax.fori_loop(1, n_frames, greet, 0)
    for k in range(1, n_coils):
        pl.semaphore_signal(
            barrier, inc=1, device_id={"frames": f, "coils": coil_peer(k)}, device_id_type=MESH
        )

    def exchange(send, recv, sems, size, me, device, split):
        def block(number):
            return send.at[number] if split else send

        def copy(k, to, slot):
            return pltpu.make_async_remote_copy(
                src_ref=block(to),
                dst_ref=recv.at[slot],
                send_sem=sems.at[0, k],
                recv_sem=sems.at[1, k],
                device_id={"frames": device(to), "coils": j},
                device_id_type=MESH,
            )

        def start():
            def body(k, _):
                copy(k, lax.rem(me + k, size), me).start()
                return 0

            lax.fori_loop(1, size, body, 0)
            recv[me] = send[me] if split else send[...]

        def wait():
            def body(k, _):
                source = lax.rem(me + size - k, size)
                copy(k, source, source).wait_recv()
                return 0

            lax.fori_loop(1, size, body, 0)

        def drain():
            def body(k, _):
                copy(k, lax.rem(me + k, size), me).wait_send()
                return 0

            lax.fori_loop(1, size, body, 0)

        return start, wait, drain

    line = (n_lines, z, lambda number: number * n_plane + q)
    plane = (n_plane, q, lambda number: z * n_plane + number)
    everyone = (n_frames, f, lambda number: number)
    raw_start, raw_wait, raw_drain = exchange(raw_send, raw_recv, raw_sems, *line, False)
    par_start, par_wait, par_drain = exchange(par_send, par_recv, par_sems, *plane, True)
    img_start, img_wait, img_drain = exchange(img_send, img_recv, img_sems, *everyone, True)
    res_start, res_wait, res_drain = exchange(res_send, res_recv, res_sems, *everyone, True)
    step_start, step_wait, step_drain = exchange(step_send, step_recv, step_sems, *everyone, False)

    loaded("ktrans", "kep", "baseline")
    folds, fold = raw_rows.shape[0] // 4, raw_rows.shape[1]
    for p, value in enumerate((ktrans[...], kep[...], baseline[0], baseline[1])):
        for i in range(folds):
            raw_rows[p * folds + i : p * folds + i + 1, :] = value[:, i * fold : (i + 1) * fold]
    raw_send[...] = raw_rows[...].astype(BF16)

    loaded("index", "offset", "count", "table")
    number = spoke_index[...]
    turn = ((number * 40503) & 65535).astype(F32) * (2.0 * math.pi / 65536.0)
    live = jnp.where(
        lax.broadcasted_iota(jnp.int32, (1, spokes), 1) < count[0], 1.0, 0.0
    ).astype(F32)
    diagonal = lax.broadcasted_iota(jnp.int32, (spokes, spokes), 0) == (
        lax.broadcasted_iota(jnp.int32, (spokes, spokes), 1)
    )

    def column(row):
        return jnp.sum(jnp.where(diagonal, row, 0.0), 1, keepdims=True)

    w_cos = column(live * jnp.cos(turn))
    w_sin = column(live * jnp.sin(turn))
    first = column(offset[...].astype(F32)).astype(jnp.int32)
    tap = lax.broadcasted_iota(jnp.int32, (spokes, width), 1) - first
    band = jnp.where(
        (tap == 0) | (tap == 3), 0.25, jnp.where((tap == 1) | (tap == 2), 0.75, 0.0)
    )
    m_cos = band * w_cos
    m_sin = band * w_sin
    m_a = jnp.concatenate([m_cos, m_sin], 0).astype(BF16)
    m_b = jnp.concatenate([-m_sin, m_cos], 0).astype(BF16)
    left[...] = (
        lax.dot_general(table[:, :width], m_a, NT, preferred_element_type=F32)
        + lax.dot_general(table[:, width:], m_b, NT, preferred_element_type=F32)
    ).astype(BF16)

    loaded("kspace")
    lines = jnp.dot(
        kspace[0].reshape(coils * 2 * spokes, width), table[...], preferred_element_type=F32
    )
    for c in range(coils):
        real = lines[2 * c * spokes : (2 * c + 1) * spokes]
        imag = lines[(2 * c + 1) * spokes : (2 * c + 2) * spokes]
        h_r = (real[:, :width] - imag[:, width:]).astype(BF16)
        h_i = (real[:, width:] + imag[:, :width]).astype(BF16)
        at = 2 * c * width
        right[:spokes, at : at + width] = h_r
        right[:spokes, at + width : at + 2 * width] = h_i
        right[spokes:, at : at + width] = -h_i
        right[spokes:, at + width : at + 2 * width] = h_r

    def partial(which):
        top = pl.multiple_of(which * rows, rows)
        coil_image = jnp.dot(
            left[pl.ds(top, rows), :], right[...], preferred_element_type=F32
        )
        image_r = jnp.zeros((rows, width), F32)
        image_i = jnp.zeros((rows, width), F32)
        for c in range(coils):
            s_r = sens[c, 0, pl.ds(top, rows), :].astype(F32)
            s_i = sens[c, 1, pl.ds(top, rows), :].astype(F32)
            c_r = coil_image[:, 2 * c * width : (2 * c + 1) * width]
            c_i = coil_image[:, (2 * c + 1) * width : (2 * c + 2) * width]
            image_r = image_r + s_r * c_r + s_i * c_i
            image_i = image_i + s_r * c_i - s_i * c_r
        return image_r, image_i

    loaded("sens")

    def part_copy(k):
        return pltpu.make_async_remote_copy(
            src_ref=part_send.at[k - 1],
            dst_ref=part_recv.at[k - 1],
            send_sem=part_sems.at[0, k],
            recv_sem=part_sems.at[1, k],
            device_id={"frames": f, "coils": coil_peer(k)},
            device_id_type=MESH,
        )

    for k in range(1, n_coils):
        image_r, image_i = partial(coil_peer(k))
        part_send[k - 1, 0] = image_r
        part_send[k - 1, 1] = image_i
    pl.semaphore_wait(barrier, n_frames + n_coils - 2)
    for k in range(1, n_coils):
        part_copy(k).start()
    raw_start()

    image_r, image_i = partial(j)

    loaded(*range(n_lines))
    place = owner[0:1, :]
    for c in range(1, n_coils):
        place = jnp.where(j == c, owner[c : c + 1, :], place)
    lo = place & (width - 1)
    hi = lax.shift_right_logical(place, int(math.log2(width)))
    own_hi[...] = hi[:, :voxels]
    for b in range(1, n_lines):
        own_hi[...] = jnp.where(z == b, hi[:, b * voxels : (b + 1) * voxels], own_hi[...])
    hi = hi - z * plane_rows
    for b in range(n_lines):
        cut = slice(b * voxels, (b + 1) * voxels)
        one_lo[:, cut] = jnp.where(
            lax.broadcasted_iota(jnp.int32, (width, voxels), 0) == lo[:, cut], 1.0, 0.0
        ).astype(BF16)

    for k in range(1, n_coils):
        part_copy(k).wait_recv()
        image_r = image_r + part_recv[k - 1, 0]
        image_i = image_i + part_recv[k - 1, 1]
    for e in range(n_frames):
        pieces = chunks.take(image_r, e) + chunks.take(image_i, e)
        img_send[e] = jnp.concatenate(pieces, 0).astype(BF16)
    img_start()

    raw_wait()
    for b in range(n_lines):
        block = raw_recv[b].astype(F32)
        for i in range(folds):
            cut = slice(b * voxels + i * fold, b * voxels + (i + 1) * fold)
            in_row = lax.broadcasted_iota(jnp.int32, (plane_rows, fold), 0) == hi[:, cut]
            spread[:, cut] = jnp.concatenate(
                [
                    jnp.where(in_row, block[p * folds + i : p * folds + i + 1], 0.0)
                    for p in range(4)
                ],
                0,
            ).astype(BF16)
    placed = lax.dot_general(spread[...], one_lo[...], NT, preferred_element_type=F32)
    for e in range(n_plane):
        pieces = []
        for p in range(4):
            pieces += chunks.take(placed[p * plane_rows : (p + 1) * plane_rows], e)
        par_send[e] = jnp.concatenate(pieces, 0).astype(BF16)
    par_start()


    par_wait()
    params = par_recv[0].astype(F32)
    for e in range(1, n_plane):
        params = params + par_recv[e].astype(F32)
    kt, kp, base_r, base_i = [params[p * height : (p + 1) * height] for p in range(4)]
    loaded("aif")
    taps = [aif[t] * STEP_MINUTES for t in range(n_frames)]
    decay = [jnp.exp(-(t * STEP_MINUTES) * kp) for t in range(n_frames)]
    drift = [decay[t] * -(t * STEP_MINUTES) for t in range(n_frames)]

    def convolve(curve, t):
        total = taps[t] * curve[0]
        for m in range(1, t + 1):
            total = total + taps[t - m] * curve[m]
        return total

    conc = [convolve(decay, t) for t in range(n_frames)]
    slope = [convolve(drift, t) for t in range(n_frames)]
    power = base_r * base_r + base_i * base_i
    h_aa = power * sum(c * c for c in conc)
    h_ab = power * kt * sum(c * s for c, s in zip(conc, slope))
    h_bb = power * kt * kt * sum(s * s for s in slope)
    d_aa = (1.0 + DAMPING) * h_aa + 1.0
    d_bb = (1.0 + DAMPING) * h_bb + 1.0
    determinant = d_aa * d_bb - h_ab * h_ab

    img_wait()
    g_a = jnp.zeros_like(kt)
    g_b = jnp.zeros_like(kt)
    for t in range(n_frames):
        image = img_recv[t].astype(F32)
        scale = 1.0 + kt * conc[t]
        project = base_r * (image[:height] - base_r * scale) + base_i * (
            image[height:] - base_i * scale
        )
        g_a = g_a + conc[t] * project
        g_b = g_b + slope[t] * project
    g_b = kt * g_b
    step_kt = (d_bb * g_a - h_ab * g_b) / determinant
    step_kp = (d_aa * g_b - h_ab * g_a) / determinant
    step_send[...] = jnp.concatenate([step_kt, step_kp], 0).astype(BF16)
    step_start()
    kt_next = kt + step_kt
    kp_next = kp + step_kp
    decay = [jnp.exp(-(t * STEP_MINUTES) * kp_next) for t in range(n_frames)]
    for t in range(n_frames):
        image = img_recv[t].astype(F32)
        scale = 1.0 + kt_next * convolve(decay, t)
        res_send[t] = jnp.concatenate(
            [image[:height] - base_r * scale, image[height:] - base_i * scale], 0
        ).astype(BF16)
    res_start()

    def unpack(block, target, number):
        at = 0
        for p in range(2):
            for row, lanes in chunks.pieces(number):
                top = p * rows + row
                target[top : top + chunks.rows, lanes] = block[at : at + chunks.rows]
                at += chunks.rows

    step_wait()
    for e in range(n_frames):
        unpack(step_recv[e].astype(F32), full, e)
    own_cut = pl.ds(pl.multiple_of(z * voxels, LANES), voxels)
    picked = jnp.dot(
        full[...].astype(BF16), one_lo[:, own_cut], preferred_element_type=F32
    )
    in_row = lax.broadcasted_iota(jnp.int32, (rows, voxels), 0) == own_hi[...]
    for p, (old, new) in enumerate(((ktrans, kt_out), (kep, kp_out))):
        new[...] = old[...] + jnp.sum(
            jnp.where(in_row, picked[p * rows : (p + 1) * rows], 0.0), 0, keepdims=True
        )

    res_wait()
    for e in range(n_frames):
        unpack(res_recv[e].astype(F32), full, e)
    for p in range(2):
        res_out[0, p] = full[p * rows : (p + 1) * rows, :].astype(BF16)
    for k in range(1, n_coils):
        part_copy(k).wait_send()
    raw_drain()
    par_drain()
    img_drain()
    step_drain()
    res_drain()


def hand_over(*refs):
    count = len(refs) // 3
    sems = refs[-1]
    into, out = [], []
    for i in range(count):
        held = refs[2 * count + i]
        into.append(pltpu.make_async_copy(refs[i], held, sems.at[0, i]))
        out.append(pltpu.make_async_copy(held, refs[count + i], sems.at[1, i]))
    for copy in into:
        copy.start()
    for i in range(count):
        into[i].wait()
        out[i].start()
    for copy in out:
        copy.wait()


def shards(
    kspace,
    sensitivity,
    spoke_count,
    spoke_index,
    band_offset,
    owner_map,
    aif,
    ktrans,
    kep,
    baseline,
):
    n_frames = lax.axis_size("frames")
    n_coils = lax.axis_size("coils")
    _, coils, _, spokes, width = kspace.shape
    voxels = ktrans.shape[1]
    rows = owner_map.shape[1] // width
    height = voxels // LANES
    n_plane = 1
    while n_plane * n_plane < n_frames:
        n_plane *= 2
    n_lines = n_frames // n_plane
    plane_rows = rows // n_lines
    folds = 4 if voxels % (4 * LANES) == 0 else 1
    vmem = pl.BlockSpec(memory_space=pltpu.VMEM)
    hbm = pl.BlockSpec(memory_space=pltpu.HBM)
    operands = (
        kspace,
        sensitivity,
        spoke_count,
        spoke_index,
        band_offset,
        owner_map,
        aif,
        ktrans,
        kep,
        baseline.reshape(2, 1, voxels),
        dft_table(width),
    )
    landing = [
        (pltpu.SMEM if x.ndim == 1 else pltpu.VMEM)(x.shape, x.dtype) for x in operands
    ]
    landing[5] = pltpu.VMEM((n_coils, n_lines * voxels), jnp.int32)
    results = pl.pallas_call(
        functools.partial(kernel, n_frames, n_coils),
        out_shape=[
            jax.ShapeDtypeStruct((1, voxels), F32),
            jax.ShapeDtypeStruct((1, voxels), F32),
            jax.ShapeDtypeStruct((1, 2, rows, width), BF16),
        ],
        in_specs=[hbm] * len(operands),
        out_specs=[vmem, vmem, vmem],
        scratch_shapes=landing
        + [
            pltpu.SemaphoreType.DMA((len(operands) - 1 + n_lines,)),
            pltpu.VMEM((4 * folds, voxels // folds), F32),
            pltpu.VMEM((4 * folds, voxels // folds), BF16),
            pltpu.VMEM((n_lines, 4 * folds, voxels // folds), BF16),
            pltpu.VMEM((width, n_lines * voxels), BF16),
            pltpu.VMEM((4 * plane_rows, n_lines * voxels), BF16),
            pltpu.VMEM((width, 2 * spokes), BF16),
            pltpu.VMEM((2 * spokes, coils * 2 * width), BF16),
            pltpu.VMEM((n_coils - 1, 2, rows, width), F32),
            pltpu.VMEM((n_coils - 1, 2, rows, width), F32),
            pltpu.VMEM((n_plane, 4 * height, LANES), BF16),
            pltpu.VMEM((n_plane, 4 * height, LANES), BF16),
            pltpu.VMEM((n_frames, 2 * height, LANES), BF16),
            pltpu.VMEM((n_frames, 2 * height, LANES), BF16),
            pltpu.VMEM((2 * height, LANES), BF16),
            pltpu.VMEM((n_frames, 2 * height, LANES), BF16),
            pltpu.VMEM((n_frames, 2 * height, LANES), BF16),
            pltpu.VMEM((n_frames, 2 * height, LANES), BF16),
            pltpu.VMEM((1, voxels), jnp.int32),
            pltpu.VMEM((2 * rows, width), F32),
            pltpu.SemaphoreType.DMA((2, n_coils)),
            pltpu.SemaphoreType.DMA((2, n_lines)),
            pltpu.SemaphoreType.DMA((2, n_plane)),
            pltpu.SemaphoreType.DMA((2, n_frames)),
            pltpu.SemaphoreType.DMA((2, n_frames)),
            pltpu.SemaphoreType.DMA((2, n_frames)),
        ],
        compiler_params=pltpu.CompilerParams(
            collective_id=0, has_side_effects=True, vmem_limit_bytes=56 * 1024 * 1024
        ),
    )(*operands)
    return pl.pallas_call(
        hand_over,
        out_shape=[jax.ShapeDtypeStruct(x.shape, x.dtype) for x in results],
        in_specs=[hbm] * len(results),
        out_specs=[hbm] * len(results),
        scratch_shapes=[pltpu.VMEM(x.shape, x.dtype) for x in results]
        + [pltpu.SemaphoreType.DMA((2, len(results)))],
        compiler_params=pltpu.CompilerParams(vmem_limit_bytes=56 * 1024 * 1024),
    )(*results)


def solution(mesh):
    in_specs = (
        P("frames", "coils", None, None, None),
        P("coils", None, None, None),
        P("frames"),
        P("frames", None),
        P("frames", None),
        P(),
        P(),
        P("coils", "frames"),
        P("coils", "frames"),
        P(None, "coils", "frames"),
    )
    out_specs = (P("coils", "frames"), P("coils", "frames"), P("frames", None, "coils", None))
    return jax.shard_map(shards, mesh=mesh, in_specs=in_specs, out_specs=out_specs, check_vma=False)
```

```python
import functools
import math

import jax
import jax.numpy as jnp
import numpy as np
from jax import lax
from jax.experimental import pallas as pl
from jax.experimental.pallas import tpu as pltpu
from jax.sharding import PartitionSpec as P

STEP_MINUTES = 0.05
DAMPING = 0.1
LANES = 128
MESH = pl.DeviceIdType.MESH
F32 = jnp.float32
BF16 = jnp.bfloat16
NT = (((1,), (1,)), ((), ()))


def dft_table(length):
    index = np.arange(length, dtype=np.int64)
    phase = (index[:, None] * index[None, :] % length) * (2.0 * math.pi / length)
    table = np.concatenate([np.cos(phase), np.sin(phase)], 1) / math.sqrt(length)
    return jnp.asarray(table.astype(np.float32)).astype(BF16)


class Chunks:
    def __init__(self, width, voxels):
        self.columns = min(width, voxels)
        self.rows = voxels // self.columns
        self.parts = width // self.columns
        self.height = voxels // LANES

    def pieces(self, number):
        row = number // self.parts * self.rows
        column = number % self.parts * self.columns
        for lane in range(0, self.columns, LANES):
            yield row, slice(column + lane, column + lane + LANES)

    def take(self, plane, number):
        return [plane[row : row + self.rows, lanes] for row, lanes in self.pieces(number)]


def kernel(
    n_frames,
    n_coils,
    kspace_in,
    sens_in,
    count_in,
    spoke_index_in,
    offset_in,
    owner_in,
    aif_in,
    ktrans_in,
    kep_in,
    baseline_in,
    table_in,
    kt_out,
    kp_out,
    res_out,
    kspace,
    sens,
    count,
    spoke_index,
    offset,
    owner,
    aif,
    ktrans,
    kep,
    baseline,
    table,
    input_sems,
    raw_rows,
    raw_send,
    raw_recv,
    one_lo,
    spread,
    left,
    right,
    part_send,
    part_recv,
    par_send,
    par_recv,
    img_send,
    img_recv,
    step_send,
    step_recv,
    res_send,
    res_recv,
    own_hi,
    full,
    part_sems,
    raw_sems,
    par_sems,
    img_sems,
    step_sems,
    res_sems,
):
    _, coils, _, spokes, width = kspace.shape
    rows = owner_in.shape[1] // width
    voxels = ktrans.shape[1]
    chunks = Chunks(width, voxels)
    height = chunks.height
    f = lax.axis_index("frames")
    j = lax.axis_index("coils")
    n_lines, n_plane = raw_recv.shape[0], par_recv.shape[0]
    plane_rows = rows // n_lines
    z, q = f // n_plane, lax.rem(f, n_plane)

    def slots(number):
        start = (number * n_plane + q) * voxels
        return pl.ds(pl.multiple_of(start, LANES), voxels)

    loads = {}
    for name, source, target in (
        ("ktrans", ktrans_in, ktrans),
        ("kep", kep_in, kep),
        ("baseline", baseline_in, baseline),
        ("table", table_in, table),
        ("index", spoke_index_in, spoke_index),
        ("offset", offset_in, offset),
        ("count", count_in, count),
        ("kspace", kspace_in, kspace),
        ("sens", sens_in, sens),
        ("aif", aif_in, aif),
        *[
            (b, owner_in.at[:, slots(b)], owner.at[:, b * voxels : (b + 1) * voxels])
            for b in range(n_lines)
        ],
    ):
        loads[name] = pltpu.make_async_copy(source, target, input_sems.at[len(loads)])
        loads[name].start()

    def loaded(*names):
        for name in names:
            loads[name].wait()

    def peer(k):
        return lax.rem(f + k, n_frames)

    def coil_peer(k):
        return lax.rem(j + k, n_coils)

    barrier = pltpu.get_barrier_semaphore()

    def greet(k, _):
        pl.semaphore_signal(
            barrier, inc=1, device_id={"frames": peer(k), "coils": j}, device_id_type=MESH
        )
        return 0

    lax.fori_loop(1, n_frames, greet, 0)
    for k in range(1, n_coils):
        pl.semaphore_signal(
            barrier, inc=1, device_id={"frames": f, "coils": coil_peer(k)}, device_id_type=MESH
        )

    def exchange(send, recv, sems, size, me, device, split):
        def block(number):
            return send.at[number] if split else send

        def copy(k, to, slot):
            return pltpu.make_async_remote_copy(
                src_ref=block(to),
                dst_ref=recv.at[slot],
                send_sem=sems.at[0, k],
                recv_sem=sems.at[1, k],
                device_id={"frames": device(to), "coils": j},
                device_id_type=MESH,
            )

        def start():
            def body(k, _):
                copy(k, lax.rem(me + k, size), me).start()
                return 0

            lax.fori_loop(1, size, body, 0)
            recv[me] = send[me] if split else send[...]

        def wait():
            def body(k, _):
                source = lax.rem(me + size - k, size)
                copy(k, source, source).wait_recv()
                return 0

            lax.fori_loop(1, size, body, 0)

        def drain():
            def body(k, _):
                copy(k, lax.rem(me + k, size), me).wait_send()
                return 0

            lax.fori_loop(1, size, body, 0)

        return start, wait, drain

    line = (n_lines, z, lambda number: number * n_plane + q)
    plane = (n_plane, q, lambda number: z * n_plane + number)
    everyone = (n_frames, f, lambda number: number)
    raw_start, raw_wait, raw_drain = exchange(raw_send, raw_recv, raw_sems, *line, False)
    par_start, par_wait, par_drain = exchange(par_send, par_recv, par_sems, *plane, True)
    img_start, img_wait, img_drain = exchange(img_send, img_recv, img_sems, *everyone, True)
    res_start, res_wait, res_drain = exchange(res_send, res_recv, res_sems, *everyone, True)
    step_start, step_wait, step_drain = exchange(step_send, step_recv, step_sems, *everyone, False)

    loaded("ktrans", "kep", "baseline")
    folds, fold = raw_rows.shape[0] // 4, raw_rows.shape[1]
    for p, value in enumerate((ktrans[...], kep[...], baseline[0], baseline[1])):
        for i in range(folds):
            raw_rows[p * folds + i : p * folds + i + 1, :] = value[:, i * fold : (i + 1) * fold]
    raw_send[...] = raw_rows[...].astype(BF16)

    loaded("index", "offset", "count", "table", "kspace")
    number = spoke_index[...]
    turn = ((number * 40503) & 65535).astype(F32) * (2.0 * math.pi / 65536.0)
    live = jnp.where(
        lax.broadcasted_iota(jnp.int32, (1, spokes), 1) < count[0], 1.0, 0.0
    ).astype(F32)
    diagonal = lax.broadcasted_iota(jnp.int32, (spokes, spokes), 0) == (
        lax.broadcasted_iota(jnp.int32, (spokes, spokes), 1)
    )

    def column(row):
        return jnp.sum(jnp.where(diagonal, row, 0.0), 1, keepdims=True)

    w_cos = column(live * jnp.cos(turn))
    w_sin = column(live * jnp.sin(turn))
    first = column(offset[...].astype(F32)).astype(jnp.int32)
    tap = lax.broadcasted_iota(jnp.int32, (spokes, width), 1) - first
    band = jnp.where(
        (tap == 0) | (tap == 3), 0.25, jnp.where((tap == 1) | (tap == 2), 0.75, 0.0)
    )
    m_cos = band * w_cos
    m_sin = band * w_sin
    m_a = jnp.concatenate([m_cos, m_sin], 0).astype(BF16)
    m_b = jnp.concatenate([-m_sin, m_cos], 0).astype(BF16)
    left[...] = (
        lax.dot_general(table[:, :width], m_a, NT, preferred_element_type=F32)
        + lax.dot_general(table[:, width:], m_b, NT, preferred_element_type=F32)
    ).astype(BF16)

    lines = jnp.dot(
        kspace[0].reshape(coils * 2 * spokes, width), table[...], preferred_element_type=F32
    )
    for c in range(coils):
        real = lines[2 * c * spokes : (2 * c + 1) * spokes]
        imag = lines[(2 * c + 1) * spokes : (2 * c + 2) * spokes]
        h_r = (real[:, :width] - imag[:, width:]).astype(BF16)
        h_i = (real[:, width:] + imag[:, :width]).astype(BF16)
        at = 2 * c * width
        right[:spokes, at : at + width] = h_r
        right[:spokes, at + width : at + 2 * width] = h_i
        right[spokes:, at : at + width] = -h_i
        right[spokes:, at + width : at + 2 * width] = h_r

    def partial(which):
        top = pl.multiple_of(which * rows, rows)
        coil_image = jnp.dot(
            left[pl.ds(top, rows), :], right[...], preferred_element_type=F32
        )
        image_r = jnp.zeros((rows, width), F32)
        image_i = jnp.zeros((rows, width), F32)
        for c in range(coils):
            s_r = sens[c, 0, pl.ds(top, rows), :].astype(F32)
            s_i = sens[c, 1, pl.ds(top, rows), :].astype(F32)
            c_r = coil_image[:, 2 * c * width : (2 * c + 1) * width]
            c_i = coil_image[:, (2 * c + 1) * width : (2 * c + 2) * width]
            image_r = image_r + s_r * c_r + s_i * c_i
            image_i = image_i + s_r * c_i - s_i * c_r
        return image_r, image_i

    loaded("sens")

    def part_copy(k):
        return pltpu.make_async_remote_copy(
            src_ref=part_send.at[k - 1],
            dst_ref=part_recv.at[k - 1],
            send_sem=part_sems.at[0, k],
            recv_sem=part_sems.at[1, k],
            device_id={"frames": f, "coils": coil_peer(k)},
            device_id_type=MESH,
        )

    for k in range(1, n_coils):
        image_r, image_i = partial(coil_peer(k))
        part_send[k - 1, 0] = image_r
        part_send[k - 1, 1] = image_i
    pl.semaphore_wait(barrier, n_frames + n_coils - 2)
    for k in range(1, n_coils):
        part_copy(k).start()
    raw_start()

    image_r, image_i = partial(j)

    loaded(*range(n_lines))
    place = owner[0:1, :]
    for c in range(1, n_coils):
        place = jnp.where(j == c, owner[c : c + 1, :], place)
    lo = place & (width - 1)
    hi = lax.shift_right_logical(place, int(math.log2(width)))
    own_hi[...] = hi[:, :voxels]
    for b in range(1, n_lines):
        own_hi[...] = jnp.where(z == b, hi[:, b * voxels : (b + 1) * voxels], own_hi[...])
    hi = hi - z * plane_rows
    for b in range(n_lines):
        cut = slice(b * voxels, (b + 1) * voxels)
        one_lo[:, cut] = jnp.where(
            lax.broadcasted_iota(jnp.int32, (width, voxels), 0) == lo[:, cut], 1.0, 0.0
        ).astype(BF16)

    for k in range(1, n_coils):
        part_copy(k).wait_recv()
        image_r = image_r + part_recv[k - 1, 0]
        image_i = image_i + part_recv[k - 1, 1]
    for e in range(n_frames):
        pieces = chunks.take(image_r, e) + chunks.take(image_i, e)
        img_send[e] = jnp.concatenate(pieces, 0).astype(BF16)
    img_start()

    raw_wait()
    for b in range(n_lines):
        block = raw_recv[b].astype(F32)
        for i in range(folds):
            cut = slice(b * voxels + i * fold, b * voxels + (i + 1) * fold)
            in_row = lax.broadcasted_iota(jnp.int32, (plane_rows, fold), 0) == hi[:, cut]
            spread[:, cut] = jnp.concatenate(
                [
                    jnp.where(in_row, block[p * folds + i : p * folds + i + 1], 0.0)
                    for p in range(4)
                ],
                0,
            ).astype(BF16)
    placed = lax.dot_general(one_lo[...], spread[...], NT, preferred_element_type=F32).T
    for e in range(n_plane):
        pieces = []
        for p in range(4):
            pieces += chunks.take(placed[p * plane_rows : (p + 1) * plane_rows], e)
        par_send[e] = jnp.concatenate(pieces, 0).astype(BF16)
    par_start()


    par_wait()
    params = par_recv[0].astype(F32)
    for e in range(1, n_plane):
        params = params + par_recv[e].astype(F32)
    kt, kp, base_r, base_i = [params[p * height : (p + 1) * height] for p in range(4)]
    loaded("aif")
    taps = [aif[t] * STEP_MINUTES for t in range(n_frames)]
    decay = [jnp.exp(-(t * STEP_MINUTES) * kp) for t in range(n_frames)]
    drift = [decay[t] * -(t * STEP_MINUTES) for t in range(n_frames)]

    def convolve(curve, t):
        total = taps[t] * curve[0]
        for m in range(1, t + 1):
            total = total + taps[t - m] * curve[m]
        return total

    conc = [convolve(decay, t) for t in range(n_frames)]
    slope = [convolve(drift, t) for t in range(n_frames)]
    power = base_r * base_r + base_i * base_i
    h_aa = power * sum(c * c for c in conc)
    h_ab = power * kt * sum(c * s for c, s in zip(conc, slope))
    h_bb = power * kt * kt * sum(s * s for s in slope)
    d_aa = (1.0 + DAMPING) * h_aa + 1.0
    d_bb = (1.0 + DAMPING) * h_bb + 1.0
    determinant = d_aa * d_bb - h_ab * h_ab

    img_wait()
    g_a = jnp.zeros_like(kt)
    g_b = jnp.zeros_like(kt)
    for t in range(n_frames):
        image = img_recv[t].astype(F32)
        scale = 1.0 + kt * conc[t]
        project = base_r * (image[:height] - base_r * scale) + base_i * (
            image[height:] - base_i * scale
        )
        g_a = g_a + conc[t] * project
        g_b = g_b + slope[t] * project
    g_b = kt * g_b
    step_kt = (d_bb * g_a - h_ab * g_b) / determinant
    step_kp = (d_aa * g_b - h_ab * g_a) / determinant
    step_send[...] = jnp.concatenate([step_kt, step_kp], 0).astype(BF16)
    step_start()
    kt_next = kt + step_kt
    kp_next = kp + step_kp
    decay = [jnp.exp(-(t * STEP_MINUTES) * kp_next) for t in range(n_frames)]
    for t in range(n_frames):
        image = img_recv[t].astype(F32)
        scale = 1.0 + kt_next * convolve(decay, t)
        res_send[t] = jnp.concatenate(
            [image[:height] - base_r * scale, image[height:] - base_i * scale], 0
        ).astype(BF16)
    res_start()

    def unpack(block, target, number):
        at = 0
        for p in range(2):
            for row, lanes in chunks.pieces(number):
                top = p * rows + row
                target[top : top + chunks.rows, lanes] = block[at : at + chunks.rows]
                at += chunks.rows

    step_wait()
    for e in range(n_frames):
        unpack(step_recv[e].astype(F32), full, e)
    own_cut = pl.ds(pl.multiple_of(z * voxels, LANES), voxels)
    picked = jnp.dot(
        full[...].astype(BF16), one_lo[:, own_cut], preferred_element_type=F32
    )
    in_row = lax.broadcasted_iota(jnp.int32, (rows, voxels), 0) == own_hi[...]
    for p, (old, new) in enumerate(((ktrans, kt_out), (kep, kp_out))):
        new[...] = old[...] + jnp.sum(
            jnp.where(in_row, picked[p * rows : (p + 1) * rows], 0.0), 0, keepdims=True
        )

    res_wait()
    for e in range(n_frames):
        unpack(res_recv[e].astype(F32), full, e)
    for p in range(2):
        res_out[0, p] = full[p * rows : (p + 1) * rows, :].astype(BF16)
    for k in range(1, n_coils):
        part_copy(k).wait_send()
    raw_drain()
    par_drain()
    img_drain()
    step_drain()
    res_drain()


def hand_over(*refs):
    count = len(refs) // 3
    sems = refs[-1]
    into, out = [], []
    for i in range(count):
        held = refs[2 * count + i]
        into.append(pltpu.make_async_copy(refs[i], held, sems.at[0, i]))
        out.append(pltpu.make_async_copy(held, refs[count + i], sems.at[1, i]))
    for copy in into:
        copy.start()
    for i in range(count):
        into[i].wait()
        out[i].start()
    for copy in out:
        copy.wait()


def shards(
    kspace,
    sensitivity,
    spoke_count,
    spoke_index,
    band_offset,
    owner_map,
    aif,
    ktrans,
    kep,
    baseline,
):
    n_frames = lax.axis_size("frames")
    n_coils = lax.axis_size("coils")
    _, coils, _, spokes, width = kspace.shape
    voxels = ktrans.shape[1]
    rows = owner_map.shape[1] // width
    height = voxels // LANES
    n_plane = 1
    while n_plane * n_plane < n_frames:
        n_plane *= 2
    n_lines = n_frames // n_plane
    plane_rows = rows // n_lines
    folds = 4 if voxels % (4 * LANES) == 0 else 1
    vmem = pl.BlockSpec(memory_space=pltpu.VMEM)
    hbm = pl.BlockSpec(memory_space=pltpu.HBM)
    operands = (
        kspace,
        sensitivity,
        spoke_count,
        spoke_index,
        band_offset,
        owner_map,
        aif,
        ktrans,
        kep,
        baseline.reshape(2, 1, voxels),
        dft_table(width),
    )
    landing = [
        (pltpu.SMEM if x.ndim == 1 else pltpu.VMEM)(x.shape, x.dtype) for x in operands
    ]
    landing[5] = pltpu.VMEM((n_coils, n_lines * voxels), jnp.int32)
    results = pl.pallas_call(
        functools.partial(kernel, n_frames, n_coils),
        out_shape=[
            jax.ShapeDtypeStruct((1, voxels), F32),
            jax.ShapeDtypeStruct((1, voxels), F32),
            jax.ShapeDtypeStruct((1, 2, rows, width), BF16),
        ],
        in_specs=[hbm] * len(operands),
        out_specs=[vmem, vmem, vmem],
        scratch_shapes=landing
        + [
            pltpu.SemaphoreType.DMA((len(operands) - 1 + n_lines,)),
            pltpu.VMEM((4 * folds, voxels // folds), F32),
            pltpu.VMEM((4 * folds, voxels // folds), BF16),
            pltpu.VMEM((n_lines, 4 * folds, voxels // folds), BF16),
            pltpu.VMEM((width, n_lines * voxels), BF16),
            pltpu.VMEM((4 * plane_rows, n_lines * voxels), BF16),
            pltpu.VMEM((width, 2 * spokes), BF16),
            pltpu.VMEM((2 * spokes, coils * 2 * width), BF16),
            pltpu.VMEM((n_coils - 1, 2, rows, width), F32),
            pltpu.VMEM((n_coils - 1, 2, rows, width), F32),
            pltpu.VMEM((n_plane, 4 * height, LANES), BF16),
            pltpu.VMEM((n_plane, 4 * height, LANES), BF16),
            pltpu.VMEM((n_frames, 2 * height, LANES), BF16),
            pltpu.VMEM((n_frames, 2 * height, LANES), BF16),
            pltpu.VMEM((2 * height, LANES), BF16),
            pltpu.VMEM((n_frames, 2 * height, LANES), BF16),
            pltpu.VMEM((n_frames, 2 * height, LANES), BF16),
            pltpu.VMEM((n_frames, 2 * height, LANES), BF16),
            pltpu.VMEM((1, voxels), jnp.int32),
            pltpu.VMEM((2 * rows, width), F32),
            pltpu.SemaphoreType.DMA((2, n_coils)),
            pltpu.SemaphoreType.DMA((2, n_lines)),
            pltpu.SemaphoreType.DMA((2, n_plane)),
            pltpu.SemaphoreType.DMA((2, n_frames)),
            pltpu.SemaphoreType.DMA((2, n_frames)),
            pltpu.SemaphoreType.DMA((2, n_frames)),
        ],
        compiler_params=pltpu.CompilerParams(
            collective_id=0, has_side_effects=True, vmem_limit_bytes=56 * 1024 * 1024
        ),
    )(*operands)
    return pl.pallas_call(
        hand_over,
        out_shape=[jax.ShapeDtypeStruct(x.shape, x.dtype) for x in results],
        in_specs=[hbm] * len(results),
        out_specs=[hbm] * len(results),
        scratch_shapes=[pltpu.VMEM(x.shape, x.dtype) for x in results]
        + [pltpu.SemaphoreType.DMA((2, len(results)))],
        compiler_params=pltpu.CompilerParams(vmem_limit_bytes=56 * 1024 * 1024),
    )(*results)


def solution(mesh):
    in_specs = (
        P("frames", "coils", None, None, None),
        P("coils", None, None, None),
        P("frames"),
        P("frames", None),
        P("frames", None),
        P(),
        P(),
        P("coils", "frames"),
        P("coils", "frames"),
        P(None, "coils", "frames"),
    )
    out_specs = (P("coils", "frames"), P("coils", "frames"), P("frames", None, "coils", None))
    return jax.shard_map(shards, mesh=mesh, in_specs=in_specs, out_specs=out_specs, check_vma=False)
```

```python
import functools
import math

import jax
import jax.numpy as jnp
import numpy as np
from jax import lax
from jax.experimental import pallas as pl
from jax.experimental.pallas import tpu as pltpu
from jax.sharding import PartitionSpec as P

STEP_MINUTES = 0.05
DAMPING = 0.1
LANES = 128
MESH = pl.DeviceIdType.MESH
F32 = jnp.float32
BF16 = jnp.bfloat16
NT = (((1,), (1,)), ((), ()))


def dft_table(length):
    index = np.arange(length, dtype=np.int64)
    phase = (index[:, None] * index[None, :] % length) * (2.0 * math.pi / length)
    table = np.concatenate([np.cos(phase), np.sin(phase)], 1) / math.sqrt(length)
    return jnp.asarray(table.astype(np.float32)).astype(BF16)


class Chunks:
    def __init__(self, width, voxels):
        self.columns = min(width, voxels)
        self.rows = voxels // self.columns
        self.parts = width // self.columns
        self.height = voxels // LANES

    def pieces(self, number):
        row = number // self.parts * self.rows
        column = number % self.parts * self.columns
        for lane in range(0, self.columns, LANES):
            yield row, slice(column + lane, column + lane + LANES)

    def take(self, plane, number):
        return [plane[row : row + self.rows, lanes] for row, lanes in self.pieces(number)]


def kernel(
    n_frames,
    n_coils,
    kspace_in,
    sens_in,
    count_in,
    spoke_index_in,
    offset_in,
    owner_in,
    aif_in,
    ktrans_in,
    kep_in,
    baseline_in,
    table_in,
    kt_out,
    kp_out,
    res_out,
    kspace,
    sens,
    count,
    spoke_index,
    offset,
    owner,
    aif,
    ktrans,
    kep,
    baseline,
    table,
    input_sems,
    raw_rows,
    raw_send,
    raw_recv,
    one_lo,
    spread,
    left,
    right,
    part_send,
    part_recv,
    par_send,
    par_recv,
    img_send,
    img_recv,
    step_send,
    step_recv,
    res_send,
    res_recv,
    own_hi,
    full,
    part_sems,
    raw_sems,
    par_sems,
    img_sems,
    step_sems,
    res_sems,
):
    _, coils, _, spokes, width = kspace.shape
    rows = owner_in.shape[1] // width
    voxels = ktrans.shape[1]
    chunks = Chunks(width, voxels)
    height = chunks.height
    f = lax.axis_index("frames")
    j = lax.axis_index("coils")
    n_lines, n_plane = raw_recv.shape[0], par_recv.shape[0]
    plane_rows = rows // n_lines
    z, q = f // n_plane, lax.rem(f, n_plane)

    def slots(number):
        start = (number * n_plane + q) * voxels
        return pl.ds(pl.multiple_of(start, LANES), voxels)

    loads = {}
    for name, source, target in (
        ("ktrans", ktrans_in, ktrans),
        ("kep", kep_in, kep),
        ("baseline", baseline_in, baseline),
        ("table", table_in, table),
        ("index", spoke_index_in, spoke_index),
        ("offset", offset_in, offset),
        ("count", count_in, count),
        ("kspace", kspace_in, kspace),
        ("sens", sens_in, sens),
        ("aif", aif_in, aif),
        *[
            (b, owner_in.at[:, slots(b)], owner.at[:, b * voxels : (b + 1) * voxels])
            for b in range(n_lines)
        ],
    ):
        loads[name] = pltpu.make_async_copy(source, target, input_sems.at[len(loads)])
        loads[name].start()

    def loaded(*names):
        for name in names:
            loads[name].wait()

    def peer(k):
        return lax.rem(f + k, n_frames)

    def coil_peer(k):
        return lax.rem(j + k, n_coils)

    barrier = pltpu.get_barrier_semaphore()

    def greet(k, _):
        pl.semaphore_signal(
            barrier, inc=1, device_id={"frames": peer(k), "coils": j}, device_id_type=MESH
        )
        return 0

    lax.fori_loop(1, n_frames, greet, 0)
    for k in range(1, n_coils):
        pl.semaphore_signal(
            barrier, inc=1, device_id={"frames": f, "coils": coil_peer(k)}, device_id_type=MESH
        )

    def exchange(send, recv, sems, size, me, device, split):
        def block(number):
            return send.at[number] if split else send

        def copy(k, to, slot):
            return pltpu.make_async_remote_copy(
                src_ref=block(to),
                dst_ref=recv.at[slot],
                send_sem=sems.at[0, k],
                recv_sem=sems.at[1, k],
                device_id={"frames": device(to), "coils": j},
                device_id_type=MESH,
            )

        def start():
            def body(k, _):
                copy(k, lax.rem(me + k, size), me).start()
                return 0

            lax.fori_loop(1, size, body, 0)
            recv[me] = send[me] if split else send[...]

        def wait():
            def body(k, _):
                source = lax.rem(me + size - k, size)
                copy(k, source, source).wait_recv()
                return 0

            lax.fori_loop(1, size, body, 0)

        def drain():
            def body(k, _):
                copy(k, lax.rem(me + k, size), me).wait_send()
                return 0

            lax.fori_loop(1, size, body, 0)

        return start, wait, drain

    line = (n_lines, z, lambda number: number * n_plane + q)
    plane = (n_plane, q, lambda number: z * n_plane + number)
    everyone = (n_frames, f, lambda number: number)
    raw_start, raw_wait, raw_drain = exchange(raw_send, raw_recv, raw_sems, *line, False)
    par_start, par_wait, par_drain = exchange(par_send, par_recv, par_sems, *plane, True)
    img_start, img_wait, img_drain = exchange(img_send, img_recv, img_sems, *everyone, True)
    res_start, res_wait, res_drain = exchange(res_send, res_recv, res_sems, *everyone, True)
    step_start, step_wait, step_drain = exchange(step_send, step_recv, step_sems, *everyone, False)

    loaded("ktrans", "kep", "baseline")
    folds, fold = raw_rows.shape[0] // 4, raw_rows.shape[1]
    for p, value in enumerate((ktrans[...], kep[...], baseline[0], baseline[1])):
        for i in range(folds):
            raw_rows[p * folds + i : p * folds + i + 1, :] = value[:, i * fold : (i + 1) * fold]
    raw_send[...] = raw_rows[...].astype(BF16)

    loaded("index", "offset", "count", "table")
    number = spoke_index[...]
    turn = ((number * 40503) & 65535).astype(F32) * (2.0 * math.pi / 65536.0)
    live = jnp.where(
        lax.broadcasted_iota(jnp.int32, (1, spokes), 1) < count[0], 1.0, 0.0
    ).astype(F32)
    diagonal = lax.broadcasted_iota(jnp.int32, (spokes, spokes), 0) == (
        lax.broadcasted_iota(jnp.int32, (spokes, spokes), 1)
    )

    def column(row):
        return jnp.sum(jnp.where(diagonal, row, 0.0), 1, keepdims=True)

    w_cos = column(live * jnp.cos(turn))
    w_sin = column(live * jnp.sin(turn))
    first = column(offset[...].astype(F32)).astype(jnp.int32)
    tap = lax.broadcasted_iota(jnp.int32, (spokes, width), 1) - first
    band = jnp.where(
        (tap == 0) | (tap == 3), 0.25, jnp.where((tap == 1) | (tap == 2), 0.75, 0.0)
    )
    m_cos = band * w_cos
    m_sin = band * w_sin
    m_a = jnp.concatenate([m_cos, m_sin], 0).astype(BF16)
    m_b = jnp.concatenate([-m_sin, m_cos], 0).astype(BF16)
    left[...] = (
        lax.dot_general(table[:, :width], m_a, NT, preferred_element_type=F32)
        + lax.dot_general(table[:, width:], m_b, NT, preferred_element_type=F32)
    ).astype(BF16)

    loaded("kspace")
    lines = jnp.dot(
        kspace[0].reshape(coils * 2 * spokes, width), table[...], preferred_element_type=F32
    )
    for c in range(coils):
        real = lines[2 * c * spokes : (2 * c + 1) * spokes]
        imag = lines[(2 * c + 1) * spokes : (2 * c + 2) * spokes]
        h_r = (real[:, :width] - imag[:, width:]).astype(BF16)
        h_i = (real[:, width:] + imag[:, :width]).astype(BF16)
        at = 2 * c * width
        right[:spokes, at : at + width] = h_r
        right[:spokes, at + width : at + 2 * width] = h_i
        right[spokes:, at : at + width] = -h_i
        right[spokes:, at + width : at + 2 * width] = h_r

    def partial(which):
        top = pl.multiple_of(which * rows, rows)
        coil_image = jnp.dot(
            left[pl.ds(top, rows), :], right[...], preferred_element_type=F32
        )
        image_r = jnp.zeros((rows, width), F32)
        image_i = jnp.zeros((rows, width), F32)
        for c in range(coils):
            s_r = sens[c, 0, pl.ds(top, rows), :].astype(F32)
            s_i = sens[c, 1, pl.ds(top, rows), :].astype(F32)
            c_r = coil_image[:, 2 * c * width : (2 * c + 1) * width]
            c_i = coil_image[:, (2 * c + 1) * width : (2 * c + 2) * width]
            image_r = image_r + s_r * c_r + s_i * c_i
            image_i = image_i + s_r * c_i - s_i * c_r
        return image_r, image_i

    loaded("sens")

    def part_copy(k):
        return pltpu.make_async_remote_copy(
            src_ref=part_send.at[k - 1],
            dst_ref=part_recv.at[k - 1],
            send_sem=part_sems.at[0, k],
            recv_sem=part_sems.at[1, k],
            device_id={"frames": f, "coils": coil_peer(k)},
            device_id_type=MESH,
        )

    for k in range(1, n_coils):
        image_r, image_i = partial(coil_peer(k))
        part_send[k - 1, 0] = image_r
        part_send[k - 1, 1] = image_i
    pl.semaphore_wait(barrier, n_frames + n_coils - 2)
    for k in range(1, n_coils):
        part_copy(k).start()
    raw_start()

    image_r, image_i = partial(j)

    loaded(*range(n_lines))
    place = owner[0:1, :]
    for c in range(1, n_coils):
        place = jnp.where(j == c, owner[c : c + 1, :], place)
    lo = place & (width - 1)
    hi = lax.shift_right_logical(place, int(math.log2(width)))
    own_hi[...] = hi[:, :voxels]
    for b in range(1, n_lines):
        own_hi[...] = jnp.where(z == b, hi[:, b * voxels : (b + 1) * voxels], own_hi[...])
    hi = hi - z * plane_rows
    for b in range(n_lines):
        cut = slice(b * voxels, (b + 1) * voxels)
        one_lo[:, cut] = jnp.where(
            lax.broadcasted_iota(jnp.int32, (width, voxels), 0) == lo[:, cut], 1.0, 0.0
        ).astype(BF16)

    raw_wait()
    for b in range(n_lines):
        block = raw_recv[b].astype(F32)
        for i in range(folds):
            cut = slice(b * voxels + i * fold, b * voxels + (i + 1) * fold)
            in_row = lax.broadcasted_iota(jnp.int32, (plane_rows, fold), 0) == hi[:, cut]
            spread[:, cut] = jnp.concatenate(
                [
                    jnp.where(in_row, block[p * folds + i : p * folds + i + 1], 0.0)
                    for p in range(4)
                ],
                0,
            ).astype(BF16)
    placed = lax.dot_general(spread[...], one_lo[...], NT, preferred_element_type=F32)
    for e in range(n_plane):
        pieces = []
        for p in range(4):
            pieces += chunks.take(placed[p * plane_rows : (p + 1) * plane_rows], e)
        par_send[e] = jnp.concatenate(pieces, 0).astype(BF16)
    par_start()

    for k in range(1, n_coils):
        part_copy(k).wait_recv()
        image_r = image_r + part_recv[k - 1, 0]
        image_i = image_i + part_recv[k - 1, 1]
    for e in range(n_frames):
        pieces = chunks.take(image_r, e) + chunks.take(image_i, e)
        img_send[e] = jnp.concatenate(pieces, 0).astype(BF16)
    img_start()

    par_wait()
    params = par_recv[0].astype(F32)
    for e in range(1, n_plane):
        params = params + par_recv[e].astype(F32)
    kt, kp, base_r, base_i = [params[p * height : (p + 1) * height] for p in range(4)]
    loaded("aif")
    taps = [aif[t] * STEP_MINUTES for t in range(n_frames)]
    decay = [jnp.exp(-(t * STEP_MINUTES) * kp) for t in range(n_frames)]
    drift = [decay[t] * -(t * STEP_MINUTES) for t in range(n_frames)]

    def convolve(curve, t):
        total = taps[t] * curve[0]
        for m in range(1, t + 1):
            total = total + taps[t - m] * curve[m]
        return total

    conc = [convolve(decay, t) for t in range(n_frames)]
    slope = [convolve(drift, t) for t in range(n_frames)]
    power = base_r * base_r + base_i * base_i
    h_aa = power * sum(c * c for c in conc)
    h_ab = power * kt * sum(c * s for c, s in zip(conc, slope))
    h_bb = power * kt * kt * sum(s * s for s in slope)
    d_aa = (1.0 + DAMPING) * h_aa + 1.0
    d_bb = (1.0 + DAMPING) * h_bb + 1.0
    determinant = d_aa * d_bb - h_ab * h_ab

    img_wait()
    g_a = jnp.zeros_like(kt)
    g_b = jnp.zeros_like(kt)
    for t in range(n_frames):
        image = img_recv[t].astype(F32)
        scale = 1.0 + kt * conc[t]
        project = base_r * (image[:height] - base_r * scale) + base_i * (
            image[height:] - base_i * scale
        )
        g_a = g_a + conc[t] * project
        g_b = g_b + slope[t] * project
    g_b = kt * g_b
    step_kt = (d_bb * g_a - h_ab * g_b) / determinant
    step_kp = (d_aa * g_b - h_ab * g_a) / determinant
    step_send[...] = jnp.concatenate([step_kt, step_kp], 0).astype(BF16)
    step_start()
    kt_next = kt + step_kt
    kp_next = kp + step_kp
    decay = [jnp.exp(-(t * STEP_MINUTES) * kp_next) for t in range(n_frames)]
    for t in range(n_frames):
        image = img_recv[t].astype(F32)
        scale = 1.0 + kt_next * convolve(decay, t)
        res_send[t] = jnp.concatenate(
            [image[:height] - base_r * scale, image[height:] - base_i * scale], 0
        ).astype(BF16)
    res_start()

    def unpack(block, target, number):
        at = 0
        for p in range(2):
            for row, lanes in chunks.pieces(number):
                top = p * rows + row
                target[top : top + chunks.rows, lanes] = block[at : at + chunks.rows]
                at += chunks.rows

    step_wait()
    for e in range(n_frames):
        unpack(step_recv[e].astype(F32), full, e)
    own_cut = pl.ds(pl.multiple_of(z * voxels, LANES), voxels)
    picked = jnp.dot(
        full[...].astype(BF16), one_lo[:, own_cut], preferred_element_type=F32
    )
    in_row = lax.broadcasted_iota(jnp.int32, (rows, voxels), 0) == own_hi[...]
    for p, (old, new) in enumerate(((ktrans, kt_out), (kep, kp_out))):
        new[...] = old[...] + jnp.sum(
            jnp.where(in_row, picked[p * rows : (p + 1) * rows], 0.0), 0, keepdims=True
        )

    res_wait()
    for e in range(n_frames):
        unpack(res_recv[e].astype(F32), full, e)
    for p in range(2):
        res_out[0, p] = full[p * rows : (p + 1) * rows, :].astype(BF16)
    for k in range(1, n_coils):
        part_copy(k).wait_send()
    raw_drain()
    par_drain()
    img_drain()
    step_drain()
    res_drain()


def hand_over(*refs):
    count = len(refs) // 3
    sems = refs[-1]
    into, out = [], []
    for i in range(count):
        held = refs[2 * count + i]
        into.append(pltpu.make_async_copy(refs[i], held, sems.at[0, i]))
        out.append(pltpu.make_async_copy(held, refs[count + i], sems.at[1, i]))
    for copy in into:
        copy.start()
    for i in range(count):
        into[i].wait()
        out[i].start()
    for copy in out:
        copy.wait()


def shards(
    kspace,
    sensitivity,
    spoke_count,
    spoke_index,
    band_offset,
    owner_map,
    aif,
    ktrans,
    kep,
    baseline,
):
    n_frames = lax.axis_size("frames")
    n_coils = lax.axis_size("coils")
    _, coils, _, spokes, width = kspace.shape
    voxels = ktrans.shape[1]
    rows = owner_map.shape[1] // width
    height = voxels // LANES
    n_plane = 1
    while n_plane * n_plane < n_frames:
        n_plane *= 2
    n_lines = n_frames // n_plane
    plane_rows = rows // n_lines
    folds = 4 if voxels % (4 * LANES) == 0 else 1
    vmem = pl.BlockSpec(memory_space=pltpu.VMEM)
    hbm = pl.BlockSpec(memory_space=pltpu.HBM)
    operands = (
        kspace,
        sensitivity,
        spoke_count,
        spoke_index,
        band_offset,
        owner_map,
        aif,
        ktrans,
        kep,
        baseline.reshape(2, 1, voxels),
        dft_table(width),
    )
    landing = [
        (pltpu.SMEM if x.ndim == 1 else pltpu.VMEM)(x.shape, x.dtype) for x in operands
    ]
    landing[5] = pltpu.VMEM((n_coils, n_lines * voxels), jnp.int32)
    results = pl.pallas_call(
        functools.partial(kernel, n_frames, n_coils),
        out_shape=[
            jax.ShapeDtypeStruct((1, voxels), F32),
            jax.ShapeDtypeStruct((1, voxels), F32),
            jax.ShapeDtypeStruct((1, 2, rows, width), BF16),
        ],
        in_specs=[hbm] * len(operands),
        out_specs=[vmem, vmem, vmem],
        scratch_shapes=landing
        + [
            pltpu.SemaphoreType.DMA((len(operands) - 1 + n_lines,)),
            pltpu.VMEM((4 * folds, voxels // folds), F32),
            pltpu.VMEM((4 * folds, voxels // folds), BF16),
            pltpu.VMEM((n_lines, 4 * folds, voxels // folds), BF16),
            pltpu.VMEM((width, n_lines * voxels), BF16),
            pltpu.VMEM((4 * plane_rows, n_lines * voxels), BF16),
            pltpu.VMEM((width, 2 * spokes), BF16),
            pltpu.VMEM((2 * spokes, coils * 2 * width), BF16),
            pltpu.VMEM((n_coils - 1, 2, rows, width), F32),
            pltpu.VMEM((n_coils - 1, 2, rows, width), F32),
            pltpu.VMEM((n_plane, 4 * height, LANES), BF16),
            pltpu.VMEM((n_plane, 4 * height, LANES), BF16),
            pltpu.VMEM((n_frames, 2 * height, LANES), BF16),
            pltpu.VMEM((n_frames, 2 * height, LANES), BF16),
            pltpu.VMEM((2 * height, LANES), BF16),
            pltpu.VMEM((n_frames, 2 * height, LANES), BF16),
            pltpu.VMEM((n_frames, 2 * height, LANES), BF16),
            pltpu.VMEM((n_frames, 2 * height, LANES), BF16),
            pltpu.VMEM((1, voxels), jnp.int32),
            pltpu.VMEM((2 * rows, width), F32),
            pltpu.SemaphoreType.DMA((2, n_coils)),
            pltpu.SemaphoreType.DMA((2, n_lines)),
            pltpu.SemaphoreType.DMA((2, n_plane)),
            pltpu.SemaphoreType.DMA((2, n_frames)),
            pltpu.SemaphoreType.DMA((2, n_frames)),
            pltpu.SemaphoreType.DMA((2, n_frames)),
        ],
        compiler_params=pltpu.CompilerParams(
            collective_id=0, has_side_effects=True, vmem_limit_bytes=56 * 1024 * 1024
        ),
    )(*operands)
    return pl.pallas_call(
        hand_over,
        out_shape=[jax.ShapeDtypeStruct(x.shape, x.dtype) for x in results],
        in_specs=[hbm] * len(results),
        out_specs=[hbm] * len(results),
        scratch_shapes=[pltpu.VMEM(x.shape, x.dtype) for x in results]
        + [pltpu.SemaphoreType.DMA((2, len(results)))],
        compiler_params=pltpu.CompilerParams(vmem_limit_bytes=56 * 1024 * 1024),
    )(*results)


def solution(mesh):
    in_specs = (
        P("frames", "coils", None, None, None),
        P("coils", None, None, None),
        P("frames"),
        P("frames", None),
        P("frames", None),
        P(),
        P(),
        P("coils", "frames"),
        P("coils", "frames"),
        P(None, "coils", "frames"),
    )
    out_specs = (P("coils", "frames"), P("coils", "frames"), P("frames", None, "coils", None))
    return jax.shard_map(shards, mesh=mesh, in_specs=in_specs, out_specs=out_specs, check_vma=False)
```
